512 devices in a mesh: rep: 8 (over x, core), grp: 8 (over y, z_hi), sub: 8 (over z_lo).
Axes of the slice: x: 4, y: 4, z: 16 (z_hi: 2, z_lo: 8; z = z_hi * 8 + z_lo), core: 2. Of those that a mesh axis runs over, the one named last changes fastest.
Arguments:
- table_rows: bfloat16 [48, 2048, 128], P('grp', 'sub'), may hold values from -3 to 3
- bag_rows: int32 [8192, 48, 8], P('rep', 'grp'), may hold values from 0 to 2047
- bag_lens: int32 [8192, 48], P('rep', 'grp'), may hold values from 1 to 8, 192 in all within a row
- labels: float32 [8192], P(('rep', 'grp', 'sub')), may hold values from 0 to 1
- proj: bfloat16 [2, 48, 8], replicated, may hold values from -0.875 to 0.875
- mlp_in: bfloat16 [2, 384, 384], replicated, may hold values from -0.3125 to 0.3125
- mlp_out: bfloat16 [2, 384, 1536], replicated, may hold values from -0.3125 to 0.3125
- compress: bfloat16 [2, 36, 48], replicated, may hold values from -0.875 to 0.875
- gain_fm: float32 [2, 384], replicated, may hold values from 0.25 to 1.75
- gain_out: float32 [2, 128], replicated, may hold values from 0.25 to 1.75
- head: bfloat16 [48, 128], replicated, may hold values from -0.078125 to 0.078125
Outputs:
- example_loss: float32 [8192], P(('rep', 'grp', 'sub'))
- row_grads: float32 [48, 2048, 128], P('grp', 'sub')
The draws below stay inside these ranges and needn't reach their ends.
Inputs may be any that keep to these rules, and one draw needn't show every extreme that they name: `bag_lens`: the bag sizes of one example over its 48 tables sum to 192.
All inputs are finite; a program needn't handle non-finite values. No bound on the sum of `bag_lens` on one device may be relied on, other than what follows from the above.
Results may differ from the reference program's by a relative error of at most 0.022.
Values may be sent and summed in bfloat16 or wider, within the bound.
No kernel may reach another device: no remote copies, remote signals or barrier semaphores. Data moves between devices by JAX's collectives and lax.ppermute only.
A program may use at most 64 MiB of HBM per device.

```python
import math
import jax
import jax.numpy as jnp
import numpy as np
from jax import lax

E = 128
BAG = 8
K = 8
H = 384
LAYERS = 2
ROWS_DEV = 256
TABLES = 48
ROWS = 2048
EXAMPLES = 8192
NF = 12
NL = 36
N_SUB = 8


def set_ends(entries, own_key, low, largest):
    spot = [jax.random.randint(jax.random.fold_in(own_key, axis), (), 0, length) for axis, length in enumerate(entries.shape)]
    main_axis = entries.shape.index(max(entries.shape))
    beside = spot[:main_axis] + [(spot[main_axis] + 1) % entries.shape[main_axis]] + spot[main_axis + 1:]
    return entries.at[tuple(spot)].set(low).at[tuple(beside)].set(largest)


def steps_of(rng, dims, split, least, high):
    loudness, own = 1.0, jax.random.fold_in(rng, 6)
    for position, parts in split:
        heights = jnp.exp(jax.random.uniform(jax.random.fold_in(own, position), (parts,), jnp.float32, least / len(split), high / len(split)))
        loudness = loudness * jnp.repeat(heights, dims[position] // parts).reshape([-1 if axis == position else 1 for axis in range(len(dims))])
    return loudness


def split_up(number_of, total, limit, skew):
    loads = [(1 << 20) // math.isqrt(standing ** skew) + 1 for standing in range(2, number_of + 1)]
    spare, holding = total - limit - (number_of - 1), [1] * (number_of - 1)
    while spare > 0:
        candidates = [i for i in range(number_of - 1) if holding[i] < limit]
        mass, left = sum([loads[i] for i in candidates]), spare
        for i in candidates:
            extra = min(limit - holding[i], max(1, left * loads[i] // mass), spare)
            holding[i] = holding[i] + extra
            spare = spare - extra
    return np.array([limit] + holding)


def ragged_sizes(key, count, total, limit, lean):
    if count == 2:
        one = jax.random.randint(key, (), max(1, total - limit), min(limit, total - 1) + 1)
        return jnp.stack([one, total - one])
    tallies = jnp.asarray(split_up(count, total, limit, lean), jnp.int32)
    pairs = (count - 1) // 2
    giver, sink = tallies[1:1 + 2 * pairs:2], tallies[2:2 + 2 * pairs:2]
    margin = jnp.minimum(giver - 1, limit - sink)
    moved = jax.random.randint(jax.random.fold_in(key, 1), (pairs,), 0, 1 << 20) % (margin + 1)
    tallies = tallies.at[1:1 + 2 * pairs:2].set(giver - moved).at[2:2 + 2 * pairs:2].set(sink + moved)
    return tallies[jax.random.permutation(jax.random.fold_in(key, 2), count)]


def gaussian(rng, dims, scale, most, cuts=(), kind=jnp.bfloat16):
    values = scale * jax.random.normal(rng, dims, jnp.float32)
    if cuts:
        values = values * steps_of(rng, dims, cuts, -0.22, 0.18)
    return jnp.clip(values, -most, most).astype(kind)


def setup_inputs(seed: int = 0) -> dict:
    keys = jax.random.split(jax.random.key(seed), 12)
    table_rows = gaussian(keys[0], (TABLES, ROWS, E), 0.5, 3.0, ((0, 8), (1, 8)))
    bag_rows = set_ends(jax.random.randint(keys[1], (EXAMPLES, TABLES, BAG), 0, ROWS), jax.random.fold_in(keys[1], 1), 0, ROWS - 1).astype(jnp.int32)
    bag_lens = jax.vmap(lambda own: ragged_sizes(own, TABLES, TABLES * BAG // 2, BAG, 2))(jax.random.split(keys[2], EXAMPLES)).reshape((EXAMPLES, TABLES)).astype(jnp.int32)
    labels = jnp.clip(1.0 * jax.random.uniform(keys[3], (EXAMPLES,), jnp.float32) ** steps_of(keys[3], (EXAMPLES,), ((0, 512),), -0.2, 0.2), 0.0, 1.0)
    proj = gaussian(keys[4], (LAYERS, TABLES, K), TABLES ** -0.5, 0.875)
    mlp_in = gaussian(keys[5], (LAYERS, TABLES * K, H), (TABLES * K) ** -0.5, 0.3125)
    mlp_out = gaussian(keys[6], (LAYERS, H, NF * E), H ** -0.5, 0.3125)
    compress = gaussian(keys[7], (LAYERS, NL, TABLES), TABLES ** -0.5, 0.875)
    gain_fm = jnp.clip(1.0 + 0.15 * jax.random.normal(keys[8], (LAYERS, TABLES * K), jnp.float32), 0.25, 1.75)
    gain_out = jnp.clip(1.0 + 0.15 * jax.random.normal(keys[9], (LAYERS, E), jnp.float32), 0.25, 1.75)
    head = gaussian(keys[10], (TABLES, E), (TABLES * E) ** -0.5, 0.078125)
    return {"table_rows": table_rows, "bag_rows": bag_rows, "bag_lens": bag_lens, "labels": labels, "proj": proj, "mlp_in": mlp_in, "mlp_out": mlp_out, "compress": compress, "gain_fm": gain_fm, "gain_out": gain_out, "head": head}


def layer_norm(values, gain):
    center = lax.optimization_barrier(jnp.mean(values, axis=-1, keepdims=True))
    spread = lax.optimization_barrier(jnp.mean(jnp.square(values - center), axis=-1, keepdims=True))
    return (values - center) * lax.rsqrt(spread + 1e-05) * gain

def wukong_layer(features, proj, mlp_in, mlp_out, compress, gain_fm, gain_out):
    batch, fields, width = features.shape
    wide = features.astype(jnp.float32)
    summary = jnp.einsum('bne,nk->bke', wide, proj.astype(jnp.float32), precision=lax.Precision.HIGHEST).astype(jnp.bfloat16)
    pairwise = jnp.einsum('bne,bke->bnk', wide, summary.astype(jnp.float32), precision=lax.Precision.HIGHEST)
    normed = layer_norm(pairwise.reshape(batch, -1), gain_fm).astype(jnp.bfloat16)
    hidden = jax.nn.silu(jnp.dot(normed, mlp_in, preferred_element_type=jnp.float32)).astype(jnp.bfloat16)
    machine = jnp.dot(hidden, mlp_out, preferred_element_type=jnp.float32).reshape(batch, -1, width)
    linear = jnp.einsum('ln,bne->ble', compress.astype(jnp.float32), wide, precision=lax.Precision.HIGHEST)
    total = jnp.concatenate([machine, linear], axis=1) + wide
    return layer_norm(total, gain_out).astype(jnp.bfloat16)

def example_losses(features, labels, proj, mlp_in, mlp_out, compress, gain_fm, gain_out, head):
    for layer in range(proj.shape[0]):
        features = wukong_layer(features, proj[layer], mlp_in[layer], mlp_out[layer], compress[layer], gain_fm[layer], gain_out[layer])
    logit = lax.optimization_barrier(jnp.sum(features.astype(jnp.float32) * head.astype(jnp.float32), axis=(1, 2)))
    return jax.nn.softplus(logit) - labels * logit

def reference(table_rows, bag_rows, bag_lens, labels, proj, mlp_in, mlp_out, compress, gain_fm, gain_out, head):
    slots = jnp.arange(BAG, dtype=jnp.int32)
    shard_ids = jnp.arange(N_SUB, dtype=jnp.int32)

    def pool_table(operands):
        table, rows_of, sizes = operands
        live = (slots[None, :] < sizes[:, None]).astype(jnp.float32)
        fetched = table[rows_of].astype(jnp.float32) * live[:, :, None]
        owner = rows_of // ROWS_DEV
        onehot = (owner[:, :, None] == shard_ids[None, None, :]).astype(jnp.float32)
        part = jnp.einsum('ebs,ebd->esd', onehot, fetched, precision=lax.Precision.HIGHEST).astype(jnp.bfloat16)
        return lax.optimization_barrier(jnp.sum(part.astype(jnp.float32), axis=1)).astype(jnp.bfloat16)
    pooled = lax.map(pool_table, (table_rows, jnp.transpose(bag_rows, (1, 0, 2)), jnp.transpose(bag_lens)))
    features = jnp.transpose(pooled, (1, 0, 2))

    def forward(values):
        return example_losses(values, labels, proj, mlp_in, mlp_out, compress, gain_fm, gain_out, head)
    losses, pull_back = jax.vjp(forward, features)
    feature_grads = pull_back(jnp.ones_like(losses))[0]

    def table_grads(operands):
        rows_of, sizes, grads = operands
        live = (slots[None, :] < sizes[:, None]).astype(jnp.float32)
        terms = grads.astype(jnp.float32)[:, None, :] * live[:, :, None]
        empty = jnp.zeros((ROWS, E), jnp.float32)
        return empty.at[rows_of.reshape(-1)].add(terms.reshape(-1, E))
    row_grads = lax.map(table_grads, (jnp.transpose(bag_rows, (1, 0, 2)), jnp.transpose(bag_lens), jnp.transpose(feature_grads, (1, 0, 2))))
    return (losses, row_grads)
```

```python
import functools

import jax
import jax.numpy as jnp
from jax import lax
from jax.experimental import pallas as pl
from jax.experimental.pallas import tpu as pltpu
from jax.sharding import Mesh
from jax.sharding import PartitionSpec as P

REP = ("x", "core")
GRP = ("y", "zhi")
DEAD = 4095


def layer_norm(values, gain):
    center = jnp.mean(values, axis=-1, keepdims=True)
    spread = jnp.mean(jnp.square(values - center), axis=-1, keepdims=True)
    return (values - center) * lax.rsqrt(spread + 1e-05) * gain


def wukong_layer(features, proj, mlp_in, mlp_out, compress, gain_fm, gain_out):
    batch, fields, width = features.shape
    wide = features.astype(jnp.float32)
    summary = jnp.einsum(
        "bne,nk->bke", wide, proj.astype(jnp.float32), precision=lax.Precision.HIGHEST
    ).astype(jnp.bfloat16)
    pairwise = jnp.einsum(
        "bne,bke->bnk", wide, summary.astype(jnp.float32), precision=lax.Precision.HIGHEST
    )
    normed = layer_norm(pairwise.reshape(batch, -1), gain_fm).astype(jnp.bfloat16)
    hidden = jax.nn.silu(jnp.dot(normed, mlp_in, preferred_element_type=jnp.float32)).astype(
        jnp.bfloat16
    )
    machine = jnp.dot(hidden, mlp_out, preferred_element_type=jnp.float32).reshape(batch, -1, width)
    linear = jnp.einsum(
        "ln,bne->ble", compress.astype(jnp.float32), wide, precision=lax.Precision.HIGHEST
    )
    total = jnp.concatenate([machine, linear], axis=1) + wide
    return layer_norm(total, gain_out).astype(jnp.bfloat16)


def example_losses(features, labels, proj, mlp_in, mlp_out, compress, gain_fm, gain_out, head):
    for layer in range(proj.shape[0]):
        features = wukong_layer(
            features,
            proj[layer],
            mlp_in[layer],
            mlp_out[layer],
            compress[layer],
            gain_fm[layer],
            gain_out[layer],
        )
    logit = jnp.sum(features.astype(jnp.float32) * head.astype(jnp.float32), axis=(1, 2))
    return jax.nn.softplus(logit) - labels * logit


def pick_kernel(sub_ref, rows_ref, lens_ref, out_ref):
    tables, bag, _ = rows_ref.shape
    slots = lax.broadcasted_iota(jnp.int32, (bag, 128), 0)
    lanes = lax.broadcasted_iota(jnp.int32, (bag, 128), 1)
    sub = sub_ref[0]
    for table in range(tables):
        kept = jnp.zeros((bag, 128), jnp.int32)
        for run in range(8):
            cut = slice(run * 128, run * 128 + 128)
            coded = jnp.where(
                slots < lens_ref[table : table + 1, cut], rows_ref[table, :, cut], DEAD
            )
            moved = pltpu.roll(coded, (run * 16 - sub * 16) & 127, 1)
            kept = jnp.where(lanes // 16 == run, moved, kept)
        out_ref[pl.ds(table * bag, bag), :] = kept


def pool_kernel(rep_ref, bags_ref, tab_ref, pools_ref, counts_ref, idx_ref):
    reps, coded_rows, _ = bags_ref.shape
    shards, tables, rows, width = tab_ref.shape
    local = shards * rows
    rep = rep_ref[0]
    for src in range(reps):
        coded = bags_ref[src]
        mine = ((coded >> 5) & 7) == rep
        spot = ((coded >> 8) << 5) | (coded & 31)
        idx_ref[:, src * 128 : src * 128 + 128] = jnp.where(mine, spot, 1024).astype(jnp.float32)
    ids = [
        (lax.broadcasted_iota(jnp.int32, (16, 128), 0) + 16 * i).astype(jnp.float32).astype(jnp.bfloat16)
        for i in range(local // 16)
    ]
    one = jnp.ones((16, 128), jnp.bfloat16)
    zero = jnp.zeros((16, 128), jnp.bfloat16)

    def per_table(table, carry):
        for src in range(reps):
            cut = slice(src * 128, src * 128 + 128)
            slots = idx_ref[pl.ds(pl.multiple_of(table * 8, 8), 8), cut]
            keys = [
                jnp.broadcast_to(slots[b : b + 1], (16, 128)).astype(jnp.bfloat16) for b in range(8)
            ]
            for i in range(local // 16):
                hits = [jnp.where(keys[b] == ids[i], one, zero) for b in range(8)]
                while len(hits) > 1:
                    hits = [hits[k] + hits[k + 1] for k in range(0, len(hits), 2)]
                counts_ref[table, i * 16 : i * 16 + 16, cut] = hits[0]
        part = lax.dot_general(
            counts_ref[table],
            tab_ref[:, table].reshape(local, width),
            (((0,), (0,)), ((), ())),
            preferred_element_type=jnp.float32,
        )
        pools_ref[:, table] = part.astype(jnp.bfloat16).reshape(32, 32, width)
        return carry

    lax.fori_loop(0, tables, per_table, 0)


def grads_kernel(counts_ref, moved_ref, out_ref):
    tables, local, examples = counts_ref.shape
    shards, _, rows, width = out_ref.shape

    def per_table(table, carry):
        grads = moved_ref[:, table].reshape(examples, width)
        acc = jnp.dot(counts_ref[table], grads, preferred_element_type=jnp.float32)
        out_ref[:, table] = acc.astype(jnp.bfloat16).reshape(shards, rows, width)
        return carry

    lax.fori_loop(0, tables, per_table, 0)


def swap(values, axes):
    return lax.all_to_all(values, axes, split_axis=0, concat_axis=0, tiled=True)


def per_device(
    table_rows, bag_rows, bag_lens, labels, proj, mlp_in, mlp_out, compress, gain_fm, gain_out, head
):
    tables, rows_dev, width = table_rows.shape
    vmem = pl.BlockSpec(memory_space=pltpu.VMEM)
    smem = pl.BlockSpec(memory_space=pltpu.SMEM)
    params = pltpu.CompilerParams(vmem_limit_bytes=48 * 1024 * 1024)
    sub = lax.axis_index("sub")
    rep = lax.axis_index(REP)
    reps, subs, ys, zs = 8, 8, 4, 2
    part_rows = rows_dev // reps

    coded = pl.pallas_call(
        pick_kernel,
        out_shape=jax.ShapeDtypeStruct((tables * 8, 128), jnp.int32),
        in_specs=[smem, vmem, vmem],
        out_specs=vmem,
        compiler_params=params,
    )(sub.reshape(1), jnp.transpose(bag_rows, (1, 2, 0)), jnp.transpose(bag_lens))
    bags = swap(jnp.broadcast_to(coded, (reps, tables * 8, 128)), REP)

    part = lax.dynamic_slice_in_dim(table_rows, rep * part_rows, part_rows, axis=1)
    gathered = swap(jnp.broadcast_to(part, (subs, tables, part_rows, width)), "sub")

    pools, counts = pl.pallas_call(
        pool_kernel,
        out_shape=(
            jax.ShapeDtypeStruct((reps * ys, tables, 32, width), jnp.bfloat16),
            jax.ShapeDtypeStruct((tables, rows_dev, 1024), jnp.bfloat16),
        ),
        in_specs=[smem, vmem, vmem],
        out_specs=(vmem, vmem),
        scratch_shapes=[pltpu.VMEM((tables * 8, 1024), jnp.float32)],
        compiler_params=params,
    )(rep.reshape(1), bags, gathered)

    moved = swap(pools, REP + ("y",))
    summed = jnp.sum(
        moved.reshape(reps, ys, tables, zs, 16, width).astype(jnp.float32), axis=0
    ).astype(jnp.bfloat16)
    near = swap(jnp.transpose(summed, (2, 0, 1, 3, 4)), "zhi")
    features = jnp.transpose(near, (3, 1, 0, 2, 4)).reshape(16, ys * zs * tables, width)

    def forward(values):
        return example_losses(
            values, labels, proj, mlp_in, mlp_out, compress, gain_fm, gain_out, head
        )

    losses, pull_back = jax.vjp(forward, features)
    feature_grads = pull_back(jnp.ones_like(losses))[0]

    back = jnp.transpose(feature_grads.reshape(16, ys, zs, tables, width), (2, 1, 3, 0, 4))
    back = swap(back, "zhi")
    back = jnp.transpose(back, (1, 2, 0, 3, 4)).reshape(ys, tables, 32, width)
    returned = swap(
        jnp.broadcast_to(back, (reps, ys, tables, 32, width)).reshape(
            reps * ys, tables, 32, width
        ),
        REP + ("y",),
    )
    partial = pl.pallas_call(
        grads_kernel,
        out_shape=jax.ShapeDtypeStruct((subs, tables, part_rows, width), jnp.bfloat16),
        in_specs=[vmem, vmem],
        out_specs=vmem,
        compiler_params=params,
    )(counts, returned)
    pieces = swap(partial, "sub")
    own = jnp.sum(pieces.astype(jnp.float32), axis=0).astype(jnp.bfloat16)
    spread = swap(jnp.broadcast_to(own, (reps, tables, part_rows, width)), REP)
    row_grads = jnp.transpose(spread, (1, 0, 2, 3)).reshape(tables, rows_dev, width)
    return (losses, row_grads.astype(jnp.float32))


def solution(mesh):
    view = Mesh(mesh.devices.reshape(4, 2, 4, 2, 8), ("x", "core", "y", "zhi", "sub"))
    return jax.shard_map(
        per_device,
        mesh=view,
        in_specs=(
            P(GRP, "sub", None),
            P(REP, GRP, None),
            P(REP, GRP),
            P(REP + GRP + ("sub",)),
            P(),
            P(),
            P(),
            P(),
            P(),
            P(),
            P(),
        ),
        out_specs=(P(REP + GRP + ("sub",)), P(GRP, "sub", None)),
        check_vma=False,
    )
```

```python
import jax
import jax.numpy as jnp
from jax import lax
from jax.experimental import pallas as pl
from jax.experimental.pallas import tpu as pltpu
from jax.sharding import Mesh
from jax.sharding import PartitionSpec as P

REP = ("x", "core")
GRP = ("y", "zhi")
DEAD = 4095
FIELDS, BATCH, WIDTH, RANK, NF = 48, 16, 128, 8, 12
VMEM_LIMIT = 48 * 1024 * 1024


def pick_kernel(sub_ref, rows_ref, lens_ref, out_ref):
    tables, bag, _ = rows_ref.shape
    slots = lax.broadcasted_iota(jnp.int32, (bag, 128), 0)
    lanes = lax.broadcasted_iota(jnp.int32, (bag, 128), 1)
    sub = sub_ref[0]
    for table in range(tables):
        kept = jnp.zeros((bag, 128), jnp.int32)
        for run in range(8):
            cut = slice(run * 128, run * 128 + 128)
            coded = jnp.where(
                slots < lens_ref[table : table + 1, cut], rows_ref[table, :, cut], DEAD
            )
            moved = pltpu.roll(coded, (run * 16 - sub * 16) & 127, 1)
            kept = jnp.where(lanes // 16 == run, moved, kept)
        out_ref[pl.ds(table * bag, bag), :] = kept


def dot(a, b, dims):
    return lax.dot_general(a, b, (dims, ((), ())), preferred_element_type=jnp.float32)


def slide(values, shift):
    halves = []
    for half in range(2):
        part = values[half * 8 : half * 8 + 8]
        base = (shift + half * 64) % WIDTH
        if base + 7 * RANK >= WIDTH:
            part, base = pltpu.roll(part, base, 1), 0
        halves.append(pltpu.roll(part, base, 1, stride=RANK, stride_axis=0))
    return jnp.concatenate(halves, axis=0)


def dense_kernel(
    near_ref, labels_ref, mix_ref, mlp_in_ref, mlp_out_ref, gain_fm_ref, gain_out_ref, head_ref,
    loss_ref, back_ref,
    x_ref, t_ref, xhat_ref, rstd_ref, xb_ref, d_ref,
):
    f32, bf16 = jnp.float32, jnp.bfloat16
    zs, ys, tables = near_ref.shape[:3]
    layers = mix_ref.shape[0]
    block = tables * BATCH
    rows = FIELDS * BATCH
    chunk = 128
    lane = lax.broadcasted_iota(jnp.int32, (BATCH, WIDTH), 1) // RANK

    for y in range(ys):
        for z in range(zs):
            at = (y * zs + z) * block
            xb_ref[0, at : at + block] = near_ref[z, y].reshape(block, WIDTH)
    x_ref[...] = xb_ref[0].astype(f32)

    def example(ref, e):
        return ref[pl.ds(e, FIELDS, stride=BATCH), :]

    saved = []
    for layer in range(layers):
        across = jnp.concatenate([example(x_ref, e).astype(bf16) for e in range(BATCH)], axis=1)
        mixed = dot(mix_ref[layer], across, ((1,), (0,)))
        for e in range(BATCH):
            t_ref[pl.ds(e, FIELDS, stride=BATCH), :] = mixed[:, e * WIDTH : (e + 1) * WIDTH]
        pieces = [mixed[:RANK, e * WIDTH : (e + 1) * WIDTH] for e in range(BATCH)]
        summary = jnp.concatenate(pieces, axis=0).astype(bf16)
        mirrored = jnp.concatenate(pieces[::-1], axis=0).astype(bf16)
        pairs = dot(xb_ref[layer], mirrored, ((1,), (1,)))
        flat = []
        for q in range(FIELDS // BATCH):
            acc = jnp.zeros((BATCH, WIDTH), f32)
            for j in range(BATCH):
                at = (q * BATCH + j) * BATCH
                moved = slide(pairs[at : at + BATCH], (j + 1) * RANK)
                acc = jnp.where(lane == j, moved, acc)
            flat.append(acc)
        flat = jnp.concatenate(flat, axis=1)
        center = jnp.mean(flat, axis=1, keepdims=True)
        flat = flat - center
        rstd_fm = lax.rsqrt(jnp.mean(flat * flat, axis=1, keepdims=True) + 1e-05)
        nhat = flat * rstd_fm
        normed = (nhat * gain_fm_ref[layer : layer + 1]).astype(bf16)
        z = dot(normed, mlp_in_ref[layer], ((1,), (0,)))
        gate = jax.nn.sigmoid(z)
        hidden = (z * gate).astype(bf16)
        machine = dot(hidden, mlp_out_ref[layer], ((1,), (0,)))
        for n in range(NF):
            t_ref[n * BATCH : (n + 1) * BATCH] = machine[:, n * WIDTH : (n + 1) * WIDTH]
        gain = gain_out_ref[layer : layer + 1]
        for at in range(0, rows, chunk):
            cut = slice(at, at + chunk)
            total = t_ref[cut] + x_ref[cut]
            total = total - jnp.mean(total, axis=1, keepdims=True)
            rstd = lax.rsqrt(jnp.mean(total * total, axis=1, keepdims=True) + 1e-05)
            xhat = total * rstd
            xhat_ref[layer, cut] = xhat
            rstd_ref[layer, cut] = rstd
            out = (xhat * gain).astype(bf16)
            xb_ref[layer + 1, cut] = out
            x_ref[cut] = out.astype(f32)
        saved.append((summary, nhat, rstd_fm, z, gate))

    acc = jnp.zeros((BATCH, WIDTH), f32)
    head = head_ref[...].astype(f32)
    for t in range(FIELDS):
        acc = acc + x_ref[t * BATCH : (t + 1) * BATCH] * head[t : t + 1]
    logit = jnp.sum(acc, axis=1, keepdims=True)
    labels = labels_ref[...]
    loss_ref[...] = jnp.maximum(logit, 0.0) + jnp.log1p(jnp.exp(-jnp.abs(logit))) - labels * logit
    dlogit = jnp.broadcast_to(jax.nn.sigmoid(logit) - labels, (BATCH, WIDTH))
    for t in range(FIELDS):
        x_ref[t * BATCH : (t + 1) * BATCH] = (dlogit * head[t : t + 1]).astype(bf16).astype(f32)

    low = lax.broadcasted_iota(jnp.int32, (RANK, WIDTH), 0) >= NF - RANK
    for layer in reversed(range(layers)):
        summary, nhat, rstd_fm, z, gate = saved[layer]
        gain = gain_out_ref[layer : layer + 1]
        for at in range(0, rows, chunk):
            cut = slice(at, at + chunk)
            xhat = xhat_ref[layer, cut]
            dxhat = x_ref[cut] * gain
            mean_d = jnp.mean(dxhat, axis=1, keepdims=True)
            mean_p = jnp.mean(dxhat * xhat, axis=1, keepdims=True)
            t_ref[cut] = rstd_ref[layer, cut] * (dxhat - mean_d - xhat * mean_p)
        dmachine = jnp.concatenate(
            [t_ref[n * BATCH : (n + 1) * BATCH].astype(bf16) for n in range(NF)], axis=1
        )
        dhidden = dot(dmachine, mlp_out_ref[layer], ((1,), (1,))).astype(bf16).astype(f32)
        dz = (dhidden * gate * (1.0 + z * (1.0 - gate))).astype(bf16)
        dnormed = dot(dz, mlp_in_ref[layer], ((1,), (1,))).astype(bf16).astype(f32)
        dnhat = dnormed * gain_fm_ref[layer : layer + 1]
        mean_d = jnp.mean(dnhat, axis=1, keepdims=True)
        mean_p = jnp.mean(dnhat * nhat, axis=1, keepdims=True)
        dflat = rstd_fm * (dnhat - mean_d - nhat * mean_p)
        for q in range(FIELDS // BATCH):
            part = dflat[:, q * WIDTH : (q + 1) * WIDTH]
            for j in range(BATCH):
                at = (q * BATCH + j) * BATCH
                only = jnp.where(lane == j, part, 0.0)
                d_ref[at : at + BATCH] = slide(only, -j * RANK).astype(bf16)
        dpairs = d_ref[...]
        dsummary = dot(dpairs, xb_ref[layer], ((0,), (0,)))
        parts = []
        for e in range(BATCH):
            straight = example(t_ref, e)
            parts.append(
                jnp.concatenate(
                    [
                        dsummary[e * RANK : (e + 1) * RANK],
                        jnp.where(low, straight[RANK : 2 * RANK], 0.0),
                        straight[2 * RANK :],
                    ],
                    axis=0,
                ).astype(bf16)
            )
        dacross = dot(mix_ref[layer], jnp.concatenate(parts, axis=1), ((0,), (0,)))
        for e in range(BATCH):
            x_ref[pl.ds(e, FIELDS, stride=BATCH), :] = dacross[:, e * WIDTH : (e + 1) * WIDTH]
        for at in range(0, rows, chunk):
            cut = slice(at, at + chunk)
            dx = x_ref[cut] + t_ref[cut] + dot(d_ref[cut], summary, ((1,), (0,)))
            x_ref[cut] = dx.astype(bf16).astype(f32)

    for y in range(ys):
        for z in range(zs):
            at = (y * zs + z) * block
            back_ref[z, y] = x_ref[at : at + block].astype(bf16).reshape(tables, BATCH, WIDTH)


def mix_of(proj, compress):
    layers = proj.shape[0]
    gap = jnp.zeros((layers, NF - RANK, FIELDS), proj.dtype)
    return jnp.concatenate([jnp.transpose(proj, (0, 2, 1)), gap, compress], axis=1)


def counts_kernel(where_ref, b0_ref, b1_ref, b2_ref, b3_ref, counts_ref, idx_ref):
    tables, local, examples = counts_ref.shape
    column, core = where_ref[0], where_ref[1]
    for src, bags_ref in enumerate((b0_ref, b1_ref, b2_ref, b3_ref)):
        coded = bags_ref[...]
        mine = ((coded >> 6) & 3) == column
        side = ((coded >> 5) & 1) ^ core
        spot = (side << 8) | ((coded >> 8) << 5) | (coded & 31)
        spot = jnp.where(mine & (coded < DEAD), spot, -1)
        at = pl.multiple_of(((column + src) & 3) * 128, 128)
        idx_ref[:, pl.ds(at, 128)] = spot.astype(jnp.float32)
    steps = local // 32
    ids = [
        (lax.broadcasted_iota(jnp.int32, (16, 128), 0) + 16 * i)
        .astype(jnp.float32)
        .astype(jnp.bfloat16)
        for i in range(256 // 16)
    ]
    one = jnp.ones((16, 128), jnp.bfloat16)
    zero = jnp.zeros((16, 128), jnp.bfloat16)

    def per_table(table, carry):
        for run in range(examples // 128):
            cut = slice(run * 128, run * 128 + 128)
            slots = idx_ref[pl.ds(pl.multiple_of(table * 8, 8), 8), cut]
            for half in range(2):
                keys = [
                    jnp.broadcast_to(slots[b : b + 1] - 256.0 * half, (16, 128)).astype(jnp.bfloat16)
                    for b in range(8)
                ]
                for i in range(steps):
                    hits = [jnp.where(keys[b] == ids[i], one, zero) for b in range(8)]
                    while len(hits) > 1:
                        hits = [hits[k] + hits[k + 1] for k in range(0, len(hits), 2)]
                    at = half * 256 + i * 16
                    counts_ref[table, at : at + 16, cut] = hits[0]
        return carry

    lax.fori_loop(0, tables, per_table, 0)


def pool_kernel(counts_ref, mine_ref, other_ref, pools_ref):
    tables, local, examples = counts_ref.shape
    width = mine_ref.shape[-1]

    def per_table(table, carry):
        rows = jnp.concatenate(
            [ref[:, table].reshape(local // 2, width) for ref in (mine_ref, other_ref)], axis=0
        )
        part = dot(counts_ref[table], rows, ((0,), (0,)))
        pools_ref[:, table] = part.astype(jnp.bfloat16).reshape(examples // 32, 32, width)
        return carry

    lax.fori_loop(0, tables, per_table, 0)


def merge_kernel(moved_ref, out_ref):
    columns, ys, tables = moved_ref.shape[:3]

    def per_table(table, carry):
        for y in range(ys):
            total = moved_ref[0, y, table].astype(jnp.float32)
            for column in range(1, columns):
                total = total + moved_ref[column, y, table].astype(jnp.float32)
            total = total.astype(jnp.bfloat16)
            out_ref[0, y, table] = total[:BATCH]
            out_ref[1, y, table] = total[BATCH:]
        return carry

    lax.fori_loop(0, tables, per_table, 0)


def grads_kernel(counts_ref, moved_ref, mine_ref, other_ref):
    tables, local, examples = counts_ref.shape
    shards, _, rows, width = mine_ref.shape

    def per_table(table, carry):
        grads = moved_ref[:, table].reshape(examples, width)
        acc = dot(counts_ref[table], grads, ((1,), (0,))).astype(jnp.bfloat16)
        mine_ref[:, table] = acc[: local // 2].reshape(shards, rows, width)
        other_ref[:, table] = acc[local // 2 :].reshape(shards, rows, width)
        return carry

    lax.fori_loop(0, tables, per_table, 0)


def add_kernel(left_ref, right_ref, out_ref):
    for shard in range(out_ref.shape[0]):
        total = left_ref[shard].astype(jnp.float32) + right_ref[shard].astype(jnp.float32)
        out_ref[shard] = total.astype(jnp.bfloat16)


def swap(values, axes):
    return lax.all_to_all(values, axes, split_axis=0, concat_axis=0, tiled=True)


def call(kernel, out_shape, ins, args, scratch=()):
    vmem = pl.BlockSpec(memory_space=pltpu.VMEM)
    smem = pl.BlockSpec(memory_space=pltpu.SMEM)
    many = isinstance(out_shape, tuple)
    return pl.pallas_call(
        kernel,
        out_shape=out_shape,
        in_specs=[smem if kind == "s" else vmem for kind in ins],
        out_specs=(vmem,) * len(out_shape) if many else vmem,
        scratch_shapes=list(scratch),
        compiler_params=pltpu.CompilerParams(vmem_limit_bytes=VMEM_LIMIT),
    )(*args)


def per_device(
    table_rows, bag_rows, bag_lens, labels, proj, mlp_in, mlp_out, compress, gain_fm, gain_out, head
):
    f32, bf16 = jnp.float32, jnp.bfloat16
    shape = jax.ShapeDtypeStruct
    tables, rows_dev, width = table_rows.shape
    layers = proj.shape[0]
    sub = lax.axis_index("sub")
    rep = lax.axis_index(REP)
    column, core = lax.axis_index("x"), lax.axis_index("core")
    columns, cores, subs, ys, zs = 4, 2, 8, 4, 2
    reps = columns * cores
    part_rows = rows_dev // reps
    examples = columns * ys * zs * BATCH
    across = [(0, 1), (1, 0)]

    coded = call(
        pick_kernel,
        shape((tables * 8, 128), jnp.int32),
        "svv",
        (sub.reshape(1), jnp.transpose(bag_rows, (1, 2, 0)), jnp.transpose(bag_lens)),
    )
    bags = [coded] + [
        lax.ppermute(coded, "x", [((i + hop) % columns, i) for i in range(columns)])
        for hop in range(1, columns)
    ]
    part = lax.dynamic_slice_in_dim(table_rows, rep * part_rows, part_rows, axis=1)
    gathered = swap(jnp.broadcast_to(part, (subs, tables, part_rows, width)), "sub")
    counts = call(
        counts_kernel,
        shape((tables, 2 * rows_dev, examples), bf16),
        "svvvv",
        (jnp.stack([column, core]), *bags),
        [pltpu.VMEM((tables * 8, examples), f32)],
    )
    other = lax.ppermute(gathered, "core", across)
    pools = call(
        pool_kernel,
        shape((columns * ys, tables, zs * BATCH, width), bf16),
        "vvv",
        (counts, gathered, other),
    )
    moved = swap(pools, ("x", "y"))
    merged = call(
        merge_kernel,
        shape((zs, ys, tables, BATCH, width), bf16),
        "v",
        (moved.reshape(columns, ys, tables, zs * BATCH, width),),
    )
    near = swap(merged, "zhi")

    rows = FIELDS * BATCH
    losses, back = call(
        dense_kernel,
        (shape((BATCH, 1), f32), shape(near.shape, bf16)),
        "v" * 8,
        (
            near,
            labels.reshape(BATCH, 1),
            mix_of(proj, compress),
            mlp_in,
            mlp_out,
            gain_fm,
            gain_out,
            head,
        ),
        [
            pltpu.VMEM((rows, WIDTH), f32),
            pltpu.VMEM((rows, WIDTH), f32),
            pltpu.VMEM((layers, rows, WIDTH), f32),
            pltpu.VMEM((layers, rows, 1), f32),
            pltpu.VMEM((layers + 1, rows, WIDTH), bf16),
            pltpu.VMEM((rows, WIDTH), bf16),
        ],
    )

    back = jnp.transpose(swap(back, "zhi"), (1, 2, 0, 3, 4)).reshape(1, ys, tables, -1, width)
    back = jnp.broadcast_to(back, (columns, *back.shape[1:]))
    returned = swap(back.reshape(columns * ys, tables, -1, width), ("x", "y"))
    piece = shape((subs, tables, part_rows, width), bf16)
    mine, other = call(grads_kernel, (piece, piece), "vv", (counts, returned))
    other = lax.ppermute(other, "core", across)
    pieces = swap(call(add_kernel, piece, "vv", (mine, other)), "sub")
    own = jnp.sum(pieces.astype(f32), axis=0).astype(bf16)
    spread = swap(jnp.broadcast_to(own, (reps, tables, part_rows, width)), REP)
    row_grads = jnp.transpose(spread, (1, 0, 2, 3)).reshape(tables, rows_dev, width)
    return (losses.reshape(BATCH), row_grads.astype(f32))


def solution(mesh):
    view = Mesh(mesh.devices.reshape(4, 2, 4, 2, 8), ("x", "core", "y", "zhi", "sub"))
    return jax.shard_map(
        per_device,
        mesh=view,
        in_specs=(
            P(GRP, "sub", None),
            P(REP, GRP, None),
            P(REP, GRP),
            P(REP + GRP + ("sub",)),
            P(),
            P(),
            P(),
            P(),
            P(),
            P(),
            P(),
        ),
        out_specs=(P(REP + GRP + ("sub",)), P(GRP, "sub", None)),
        check_vma=False,
    )
```

```python
import jax
import jax.numpy as jnp
from jax import lax
from jax.experimental import pallas as pl
from jax.experimental.pallas import tpu as pltpu
from jax.sharding import Mesh
from jax.sharding import PartitionSpec as P

REP = ("x", "core")
GRP = ("y", "zhi")
SUB = ("sub",)
DEAD = 4095
FIELDS, BATCH, WIDTH, RANK, NF = 48, 16, 128, 8, 12
VMEM_LIMIT = 48 * 1024 * 1024


def pick_kernel(sub_ref, rows_ref, lens_ref, out_ref):
    tables, bag, _ = rows_ref.shape
    slots = lax.broadcasted_iota(jnp.int32, (bag, 128), 0)
    lanes = lax.broadcasted_iota(jnp.int32, (bag, 128), 1)
    sub = sub_ref[0]
    for table in range(tables):
        kept = jnp.zeros((bag, 128), jnp.int32)
        for run in range(8):
            cut = slice(run * 128, run * 128 + 128)
            coded = jnp.where(
                slots < lens_ref[table : table + 1, cut], rows_ref[table, :, cut], DEAD
            )
            moved = pltpu.roll(coded, (run * 16 - sub * 16) & 127, 1)
            kept = jnp.where(lanes // 16 == run, moved, kept)
        out_ref[pl.ds(table * bag, bag), :] = kept


def dot(a, b, dims):
    return lax.dot_general(a, b, (dims, ((), ())), preferred_element_type=jnp.float32)


def slide(values, shift):
    halves = []
    for half in range(2):
        part = values[half * 8 : half * 8 + 8]
        base = (shift + half * 64) % WIDTH
        if base + 7 * RANK >= WIDTH:
            part, base = pltpu.roll(part, base, 1), 0
        halves.append(pltpu.roll(part, base, 1, stride=RANK, stride_axis=0))
    return jnp.concatenate(halves, axis=0)


def dense_kernel(
    near_ref, labels_ref, mix_hbm, mlp_in_hbm, mlp_out_hbm, gain_fm_hbm, gain_out_hbm, head_hbm,
    loss_ref, back_ref,
    x_ref, t_ref, xhat_ref, rstd_ref, xb_ref, d_ref,
    mix_ref, mlp_in_ref, mlp_out_ref, gain_fm_ref, gain_out_ref, head_ref, fetch_sems,
):
    f32, bf16 = jnp.float32, jnp.bfloat16
    layers = mix_ref.shape[0]
    rows = FIELDS * BATCH
    chunk = 128
    lane = lax.broadcasted_iota(jnp.int32, (BATCH, WIDTH), 1) // RANK
    fetches = [
        pltpu.make_async_copy(source, target, fetch_sems.at[i])
        for i, (source, target) in enumerate(
            (
                (mix_hbm, mix_ref),
                (gain_fm_hbm, gain_fm_ref),
                (mlp_in_hbm, mlp_in_ref),
                (mlp_out_hbm, mlp_out_ref),
                (gain_out_hbm, gain_out_ref),
                (head_hbm, head_ref),
            )
        )
    ]
    for fetch in fetches:
        fetch.start()

    xb_ref[0] = near_ref[...].reshape(rows, WIDTH)
    x_ref[...] = xb_ref[0].astype(f32)

    def example(ref, e):
        return ref[pl.ds(e, FIELDS, stride=BATCH), :]

    saved = []
    for layer in range(layers):
        across = jnp.concatenate([example(x_ref, e).astype(bf16) for e in range(BATCH)], axis=1)
        if layer == 0:
            fetches[0].wait()
        mixed = dot(mix_ref[layer], across, ((1,), (0,)))
        for e in range(BATCH):
            t_ref[pl.ds(e, FIELDS, stride=BATCH), :] = mixed[:, e * WIDTH : (e + 1) * WIDTH]
        pieces = [mixed[:RANK, e * WIDTH : (e + 1) * WIDTH] for e in range(BATCH)]
        summary = jnp.concatenate(pieces, axis=0).astype(bf16)
        mirrored = jnp.concatenate(pieces[::-1], axis=0).astype(bf16)
        pairs = dot(xb_ref[layer], mirrored, ((1,), (1,)))
        flat = []
        for q in range(FIELDS // BATCH):
            acc = jnp.zeros((BATCH, WIDTH), f32)
            for j in range(BATCH):
                at = (q * BATCH + j) * BATCH
                moved = slide(pairs[at : at + BATCH], (j + 1) * RANK)
                acc = jnp.where(lane == j, moved, acc)
            flat.append(acc)
        flat = jnp.concatenate(flat, axis=1)
        center = jnp.mean(flat, axis=1, keepdims=True)
        flat = flat - center
        rstd_fm = lax.rsqrt(jnp.mean(flat * flat, axis=1, keepdims=True) + 1e-05)
        nhat = flat * rstd_fm
        if layer == 0:
            fetches[1].wait()
            fetches[2].wait()
        normed = (nhat * gain_fm_ref[layer : layer + 1]).astype(bf16)
        z = dot(normed, mlp_in_ref[layer], ((1,), (0,)))
        gate = jax.nn.sigmoid(z)
        hidden = (z * gate).astype(bf16)
        if layer == 0:
            fetches[3].wait()
            fetches[4].wait()
        machine = dot(hidden, mlp_out_ref[layer], ((1,), (0,)))
        for n in range(NF):
            t_ref[n * BATCH : (n + 1) * BATCH] = machine[:, n * WIDTH : (n + 1) * WIDTH]
        gain = gain_out_ref[layer : layer + 1]
        for at in range(0, rows, chunk):
            cut = slice(at, at + chunk)
            total = t_ref[cut] + x_ref[cut]
            total = total - jnp.mean(total, axis=1, keepdims=True)
            rstd = lax.rsqrt(jnp.mean(total * total, axis=1, keepdims=True) + 1e-05)
            xhat = total * rstd
            xhat_ref[layer, cut] = xhat
            rstd_ref[layer, cut] = rstd
            out = (xhat * gain).astype(bf16)
            xb_ref[layer + 1, cut] = out
            x_ref[cut] = out.astype(f32)
        saved.append((summary, nhat, rstd_fm, z, gate))

    acc = jnp.zeros((BATCH, WIDTH), f32)
    fetches[5].wait()
    head = head_ref[...].astype(f32)
    for t in range(FIELDS):
        acc = acc + x_ref[t * BATCH : (t + 1) * BATCH] * head[t : t + 1]
    logit = jnp.sum(acc, axis=1, keepdims=True)
    square = (BATCH, BATCH)
    same = lax.broadcasted_iota(jnp.int32, square, 0) == lax.broadcasted_iota(jnp.int32, square, 1)
    labels = jnp.sum(
        jnp.where(same, jnp.broadcast_to(labels_ref[...], square), 0.0), axis=1, keepdims=True
    )
    loss = jnp.maximum(logit, 0.0) + jnp.log1p(jnp.exp(-jnp.abs(logit))) - labels * logit
    loss_ref[...] = jnp.sum(
        jnp.where(same, jnp.broadcast_to(loss, square), 0.0), axis=0, keepdims=True
    )
    dlogit = jnp.broadcast_to(jax.nn.sigmoid(logit) - labels, (BATCH, WIDTH))
    for t in range(FIELDS):
        x_ref[t * BATCH : (t + 1) * BATCH] = (dlogit * head[t : t + 1]).astype(bf16).astype(f32)

    low = lax.broadcasted_iota(jnp.int32, (RANK, WIDTH), 0) >= NF - RANK
    for layer in reversed(range(layers)):
        summary, nhat, rstd_fm, z, gate = saved[layer]
        gain = gain_out_ref[layer : layer + 1]
        for at in range(0, rows, chunk):
            cut = slice(at, at + chunk)
            xhat = xhat_ref[layer, cut]
            dxhat = x_ref[cut] * gain
            mean_d = jnp.mean(dxhat, axis=1, keepdims=True)
            mean_p = jnp.mean(dxhat * xhat, axis=1, keepdims=True)
            t_ref[cut] = rstd_ref[layer, cut] * (dxhat - mean_d - xhat * mean_p)
        dmachine = jnp.concatenate(
            [t_ref[n * BATCH : (n + 1) * BATCH].astype(bf16) for n in range(NF)], axis=1
        )
        dhidden = dot(dmachine, mlp_out_ref[layer], ((1,), (1,))).astype(bf16).astype(f32)
        dz = (dhidden * gate * (1.0 + z * (1.0 - gate))).astype(bf16)
        dnormed = dot(dz, mlp_in_ref[layer], ((1,), (1,))).astype(bf16).astype(f32)
        dnhat = dnormed * gain_fm_ref[layer : layer + 1]
        mean_d = jnp.mean(dnhat, axis=1, keepdims=True)
        mean_p = jnp.mean(dnhat * nhat, axis=1, keepdims=True)
        dflat = rstd_fm * (dnhat - mean_d - nhat * mean_p)
        for q in range(FIELDS // BATCH):
            part = dflat[:, q * WIDTH : (q + 1) * WIDTH]
            for j in range(BATCH):
                at = (q * BATCH + j) * BATCH
                only = jnp.where(lane == j, part, 0.0)
                d_ref[at : at + BATCH] = slide(only, -j * RANK).astype(bf16)
        dpairs = d_ref[...]
        dsummary = dot(dpairs, xb_ref[layer], ((0,), (0,)))
        parts = []
        for e in range(BATCH):
            straight = example(t_ref, e)
            parts.append(
                jnp.concatenate(
                    [
                        dsummary[e * RANK : (e + 1) * RANK],
                        jnp.where(low, straight[RANK : 2 * RANK], 0.0),
                        straight[2 * RANK :],
                    ],
                    axis=0,
                ).astype(bf16)
            )
        dacross = dot(mix_ref[layer], jnp.concatenate(parts, axis=1), ((0,), (0,)))
        for e in range(BATCH):
            x_ref[pl.ds(e, FIELDS, stride=BATCH), :] = dacross[:, e * WIDTH : (e + 1) * WIDTH]
        for at in range(0, rows, chunk):
            cut = slice(at, at + chunk)
            dx = x_ref[cut] + t_ref[cut] + dot(d_ref[cut], summary, ((1,), (0,)))
            x_ref[cut] = dx.astype(bf16).astype(f32)

    back_ref[...] = x_ref[...].astype(bf16).reshape(back_ref.shape)


def mix_of(proj, compress):
    layers = proj.shape[0]
    gap = jnp.zeros((layers, NF - RANK, FIELDS), proj.dtype)
    return jnp.concatenate([jnp.transpose(proj, (0, 2, 1)), gap, compress], axis=1)


def counts_kernel(where_ref, b0_ref, b1_ref, b2_ref, b3_ref, counts_ref, idx_ref):
    tables, local, examples = counts_ref.shape
    column, core = where_ref[0], where_ref[1]
    for hop, bags_ref in enumerate((b0_ref, b1_ref, b2_ref, b3_ref)):
        coded = bags_ref[...]
        mine = ((coded >> 6) & 3) == column
        side = ((coded >> 5) & 1) ^ core
        spot = (side << 8) | ((coded >> 8) << 5) | (coded & 31)
        spot = jnp.where(mine & (coded < DEAD), spot, -1)
        at = pl.multiple_of(((column + hop) & 3) * 128, 128)
        idx_ref[:, pl.ds(at, 128)] = spot.astype(jnp.float32)
    steps = local // 32
    ids = [
        (lax.broadcasted_iota(jnp.int32, (16, 128), 0) + 16 * i)
        .astype(jnp.float32)
        .astype(jnp.bfloat16)
        for i in range(256 // 16)
    ]
    one = jnp.ones((16, 128), jnp.bfloat16)
    zero = jnp.zeros((16, 128), jnp.bfloat16)

    def per_table(table, carry):
        for run in range(examples // 128):
            cut = slice(run * 128, run * 128 + 128)
            slots = idx_ref[pl.ds(pl.multiple_of(table * 8, 8), 8), cut]
            for half in range(2):
                keys = [
                    jnp.broadcast_to(slots[b : b + 1] - 256.0 * half, (16, 128)).astype(jnp.bfloat16)
                    for b in range(8)
                ]
                for i in range(steps):
                    hits = [jnp.where(keys[b] == ids[i], one, zero) for b in range(8)]
                    while len(hits) > 1:
                        hits = [hits[k] + hits[k + 1] for k in range(0, len(hits), 2)]
                    at = half * 256 + i * 16
                    counts_ref[table, at : at + 16, cut] = hits[0]
        return carry

    lax.fori_loop(0, tables, per_table, 0)


def pool_kernel(counts_ref, mine_ref, other_ref, pools_ref):
    tables, local, examples = counts_ref.shape
    width = mine_ref.shape[-1]

    def per_table(table, carry):
        rows = jnp.concatenate(
            [ref[:, table].reshape(local // 2, width) for ref in (mine_ref, other_ref)], axis=0
        )
        part = dot(counts_ref[table], rows, ((0,), (0,)))
        pools_ref[:, table] = part.astype(jnp.bfloat16).reshape(examples // BATCH, BATCH, width)
        return carry

    lax.fori_loop(0, tables, per_table, 0)


def merge_kernel(moved_ref, out_ref):
    for at in range(out_ref.shape[0]):
        total = moved_ref[0, at].astype(jnp.float32)
        for source in range(1, moved_ref.shape[0]):
            total = total + moved_ref[source, at].astype(jnp.float32)
        out_ref[at] = total.astype(jnp.bfloat16)


def grads_kernel(counts_ref, moved_ref, mine_ref, other_ref):
    tables, local, examples = counts_ref.shape
    shards, _, rows, width = mine_ref.shape

    def per_table(table, carry):
        grads = moved_ref[:, table].reshape(examples, width)
        acc = dot(counts_ref[table], grads, ((1,), (0,))).astype(jnp.bfloat16)
        mine_ref[:, table] = acc[: local // 2].reshape(shards, rows, width)
        other_ref[:, table] = acc[local // 2 :].reshape(shards, rows, width)
        return carry

    lax.fori_loop(0, tables, per_table, 0)


def add_kernel(left_ref, right_ref, out_ref):
    for at in range(out_ref.shape[0]):
        total = left_ref[at].astype(jnp.float32) + right_ref[at].astype(jnp.float32)
        out_ref[at] = total.astype(jnp.bfloat16)


def swap(values, axes):
    return lax.all_to_all(values, axes, split_axis=0, concat_axis=0, tiled=True)


def call(kernel, out_shape, ins, args, scratch=(), limit=VMEM_LIMIT):
    vmem = pl.BlockSpec(memory_space=pltpu.VMEM)
    smem = pl.BlockSpec(memory_space=pltpu.SMEM)
    hbm = pl.BlockSpec(memory_space=pltpu.HBM)
    many = isinstance(out_shape, tuple)
    return pl.pallas_call(
        kernel,
        out_shape=out_shape,
        in_specs=[{"s": smem, "v": vmem, "h": hbm}[kind] for kind in ins],
        out_specs=(vmem,) * len(out_shape) if many else vmem,
        scratch_shapes=list(scratch),
        compiler_params=pltpu.CompilerParams(vmem_limit_bytes=limit),
    )(*args)


def per_device(
    table_rows, bag_rows, bag_lens, labels, proj, mlp_in, mlp_out, compress, gain_fm, gain_out, head
):
    f32, bf16 = jnp.float32, jnp.bfloat16
    shape = jax.ShapeDtypeStruct
    tables, rows_dev, width = table_rows.shape
    layers = proj.shape[0]
    rep = lax.axis_index(REP)
    sub = lax.axis_index(SUB)
    column, core = lax.axis_index("x"), lax.axis_index("core")
    columns, cores, shards, groups = 4, 2, 8, 8
    reps = columns * cores
    part_rows = rows_dev // reps
    examples = columns * groups * BATCH
    across = [(0, 1), (1, 0)]

    part = lax.dynamic_slice_in_dim(table_rows, rep * part_rows, part_rows, axis=1)
    gathered = swap(
        jnp.broadcast_to(part.reshape(1, *part.shape), (shards, tables, part_rows, width)), SUB
    )
    coded = call(
        pick_kernel,
        shape((tables * 8, 128), jnp.int32),
        "svv",
        (sub.reshape(1), jnp.transpose(bag_rows, (1, 2, 0)), jnp.transpose(bag_lens)),
    )
    bags = [coded] + [
        lax.ppermute(coded, "x", [((i + hop) % columns, i) for i in range(columns)])
        for hop in range(1, columns)
    ]
    counts = call(
        counts_kernel,
        shape((tables, 2 * rows_dev, examples), bf16),
        "svvvv",
        (jnp.stack([column, core]), *bags),
        [pltpu.VMEM((tables * 8, examples), f32)],
    )
    mix = mix_of(proj, compress)
    gathered, counts, mix = lax.optimization_barrier((gathered, counts, mix))
    other = lax.ppermute(gathered, "core", across)
    pools = call(
        pool_kernel,
        shape((columns * groups, tables, BATCH, width), bf16),
        "vvv",
        (counts, gathered, other),
    )
    moved = swap(pools, "x")
    per_group = shape((groups, tables, BATCH, width), bf16)
    merged = call(
        merge_kernel, per_group, "v", (moved.reshape(columns, groups, tables, BATCH, width),)
    )
    near = swap(merged, GRP)

    rows = FIELDS * BATCH
    losses, back = call(
        dense_kernel,
        (shape((1, BATCH), f32), shape(near.shape, bf16)),
        "vv" + "h" * 6,
        (
            near,
            labels.reshape(1, BATCH),
            mix,
            mlp_in,
            mlp_out,
            gain_fm,
            gain_out,
            head,
        ),
        [
            pltpu.VMEM((rows, WIDTH), f32),
            pltpu.VMEM((rows, WIDTH), f32),
            pltpu.VMEM((layers, rows, WIDTH), f32),
            pltpu.VMEM((layers, rows, 1), f32),
            pltpu.VMEM((layers + 1, rows, WIDTH), bf16),
            pltpu.VMEM((rows, WIDTH), bf16),
            pltpu.VMEM((layers, FIELDS, FIELDS), bf16),
            pltpu.VMEM(mlp_in.shape, bf16),
            pltpu.VMEM(mlp_out.shape, bf16),
            pltpu.VMEM(gain_fm.shape, f32),
            pltpu.VMEM(gain_out.shape, f32),
            pltpu.VMEM(head.shape, bf16),
            pltpu.SemaphoreType.DMA((6,)),
        ],
        60 * 1024 * 1024,
    )

    back = swap(back, GRP)
    back = jnp.broadcast_to(back, (columns, *back.shape))
    returned = swap(back.reshape(columns * groups, tables, BATCH, width), "x")
    piece = shape((shards, tables, part_rows, width), bf16)
    mine, other = call(grads_kernel, (piece, piece), "vv", (counts, returned))
    other = lax.ppermute(other, "core", across)
    pieces = swap(call(add_kernel, piece, "vv", (mine, other)), SUB)
    own = jnp.sum(pieces.astype(f32), axis=0).astype(bf16)
    spread = swap(jnp.broadcast_to(own, (reps, tables, part_rows, width)), REP)
    row_grads = jnp.transpose(spread, (1, 0, 2, 3)).reshape(tables, rows_dev, width)
    return (losses.reshape(BATCH), row_grads.astype(f32))


def solution(mesh):
    view = Mesh(
        mesh.devices.reshape(4, 2, 4, 2, 8), ("x", "core", "y", "zhi", "sub")
    )
    return jax.shard_map(
        per_device,
        mesh=view,
        in_specs=(
            P(GRP, SUB, None),
            P(REP, GRP, None),
            P(REP, GRP),
            P(REP + GRP + SUB),
            P(),
            P(),
            P(),
            P(),
            P(),
            P(),
            P(),
        ),
        out_specs=(P(REP + GRP + SUB), P(GRP, SUB, None)),
        check_vma=False,
    )
```

```python
import functools

import jax
import jax.numpy as jnp
from jax import lax
from jax.experimental import pallas as pl
from jax.experimental.pallas import tpu as pltpu
from jax.sharding import Mesh
from jax.sharding import PartitionSpec as P

REP = ("x", "core")
GRP = ("y", "zhi")
SUB = ("sub",)
DEAD = 4095
COLUMNS = 4
FIELDS, BATCH, WIDTH, RANK, NF = 48, 16, 128, 8, 12
VMEM_LIMIT = 24 * 1024 * 1024
DENSE_LIMIT = 56 * 1024 * 1024


def pick_kernel(where_ref, rows_hbm, lens_hbm, *refs):
    outs, (rows_ref, lens_ref, kept_ref, sems) = refs[:COLUMNS], refs[COLUMNS:]
    fetches = [
        pltpu.make_async_copy(rows_hbm, rows_ref, sems.at[0]),
        pltpu.make_async_copy(lens_hbm, lens_ref, sems.at[1]),
    ]
    for fetch in fetches:
        fetch.start()
    for fetch in fetches:
        fetch.wait()
    bag = rows_ref.shape[1]
    slots = lax.broadcasted_iota(jnp.int32, (bag, 128), 0)
    lanes = lax.broadcasted_iota(jnp.int32, (bag, 128), 1)
    sub, column = where_ref[0], where_ref[1]
    for table in range(rows_ref.shape[0]):
        kept = jnp.zeros((bag, 128), jnp.int32)
        for run in range(8):
            cut = slice(run * 128, run * 128 + 128)
            coded = jnp.where(
                slots < lens_ref[table : table + 1, cut], rows_ref[table, :, cut], DEAD
            )
            moved = pltpu.roll(coded, (run * 16 - sub * 16) & 127, 1)
            kept = jnp.where(lanes // 16 == run, moved, kept)
        kept_ref[table] = kept
    for hop in range(COLUMNS):
        target = (column - hop) & (COLUMNS - 1)
        outs[hop][:bag] = kept_ref[target]
        outs[hop][bag:] = kept_ref[COLUMNS + (target >> 1)]


def dot(a, b, dims):
    return lax.dot_general(a, b, (dims, ((), ())), preferred_element_type=jnp.float32)


def slide(values, shift):
    halves = []
    for half in range(2):
        part = values[half * 8 : half * 8 + 8]
        base = (shift + half * 64) % WIDTH
        if base + 7 * RANK >= WIDTH:
            part, base = pltpu.roll(part, base, 1), 0
        halves.append(pltpu.roll(part, base, 1, stride=RANK, stride_axis=0))
    return jnp.concatenate(halves, axis=0)


def dense_kernel(
    labels_hbm, near_hbm, mix_hbm, gain_fm_hbm, mlp_in_hbm, mlp_out_hbm, gain_out_hbm, head_hbm,
    loss_ref, back_ref,
    x_ref, t_ref, xhat_ref, rstd_ref, xb_ref, d_ref,
    near_ref, mix_ref, gain_fm_ref, mlp_in_ref, mlp_out_ref, gain_out_ref, head_ref, labels_ref, sems,
):
    f32, bf16 = jnp.float32, jnp.bfloat16
    layers = mix_ref.shape[0]
    rows = FIELDS * BATCH
    chunk = 128
    lane = lax.broadcasted_iota(jnp.int32, (BATCH, WIDTH), 1) // RANK
    pairs = (
        (near_hbm, near_ref),
        (mix_hbm, mix_ref),
        (gain_fm_hbm, gain_fm_ref),
        (mlp_in_hbm, mlp_in_ref),
        (mlp_out_hbm.at[0], mlp_out_ref.at[0]),
        (gain_out_hbm, gain_out_ref),
        (mlp_out_hbm.at[1], mlp_out_ref.at[1]),
        (head_hbm, head_ref),
        (labels_hbm, labels_ref),
    )
    fetches = [pltpu.make_async_copy(*pair, sems.at[i]) for i, pair in enumerate(pairs)]
    for fetch in fetches:
        fetch.start()

    fetches[0].wait()
    groups = near_ref.shape[1]
    tables = FIELDS // groups
    for group in range(groups):
        for table in range(tables):
            if table < COLUMNS:
                whole = near_ref[table, group, 0]
            else:
                first = 2 * (table - COLUMNS)
                whole = near_ref[first, group, 1].astype(f32) + near_ref[first + 1, group, 1].astype(f32)
            at = (group * tables + table) * BATCH
            xb_ref[0, at : at + BATCH] = whole.astype(bf16)
    x_ref[...] = xb_ref[0].astype(f32)

    def example(ref, e):
        return ref[pl.ds(e, FIELDS, stride=BATCH), :]

    saved = []
    for layer in range(layers):
        across = jnp.concatenate([example(x_ref, e).astype(bf16) for e in range(BATCH)], axis=1)
        if layer == 0:
            fetches[1].wait()
        mixed = dot(mix_ref[layer], across, ((1,), (0,)))
        for e in range(BATCH):
            t_ref[pl.ds(e, FIELDS, stride=BATCH), :] = mixed[:, e * WIDTH : (e + 1) * WIDTH]
        pieces = [mixed[:RANK, e * WIDTH : (e + 1) * WIDTH] for e in range(BATCH)]
        summary = jnp.concatenate(pieces, axis=0).astype(bf16)
        mirrored = jnp.concatenate(pieces[::-1], axis=0).astype(bf16)
        pairs = dot(xb_ref[layer], mirrored, ((1,), (1,)))
        flat = []
        for q in range(FIELDS // BATCH):
            acc = jnp.zeros((BATCH, WIDTH), f32)
            for j in range(BATCH):
                at = (q * BATCH + j) * BATCH
                moved = slide(pairs[at : at + BATCH], (j + 1) * RANK)
                acc = jnp.where(lane == j, moved, acc)
            flat.append(acc)
        flat = jnp.concatenate(flat, axis=1)
        center = jnp.mean(flat, axis=1, keepdims=True)
        flat = flat - center
        rstd_fm = lax.rsqrt(jnp.mean(flat * flat, axis=1, keepdims=True) + 1e-05)
        nhat = flat * rstd_fm
        if layer == 0:
            fetches[2].wait()
            fetches[3].wait()
        normed = (nhat * gain_fm_ref[layer : layer + 1]).astype(bf16)
        z = dot(normed, mlp_in_ref[layer], ((1,), (0,)))
        gate = jax.nn.sigmoid(z)
        hidden = (z * gate).astype(bf16)
        if layer == 0:
            fetches[4].wait()
            fetches[5].wait()
        if layer == 1:
            fetches[6].wait()
        machine = dot(hidden, mlp_out_ref[layer], ((1,), (0,)))
        for n in range(NF):
            t_ref[n * BATCH : (n + 1) * BATCH] = machine[:, n * WIDTH : (n + 1) * WIDTH]
        gain = gain_out_ref[layer : layer + 1]
        for at in range(0, rows, chunk):
            cut = slice(at, at + chunk)
            total = t_ref[cut] + x_ref[cut]
            total = total - jnp.mean(total, axis=1, keepdims=True)
            rstd = lax.rsqrt(jnp.mean(total * total, axis=1, keepdims=True) + 1e-05)
            xhat = total * rstd
            xhat_ref[layer, cut] = xhat
            rstd_ref[layer, cut] = rstd
            out = (xhat * gain).astype(bf16)
            xb_ref[layer + 1, cut] = out
            x_ref[cut] = out.astype(f32)
        saved.append((summary, nhat, rstd_fm, z, gate))

    acc = jnp.zeros((BATCH, WIDTH), f32)
    fetches[7].wait()
    fetches[8].wait()
    head = head_ref[...].astype(f32)
    for t in range(FIELDS):
        acc = acc + x_ref[t * BATCH : (t + 1) * BATCH] * head[t : t + 1]
    logit = jnp.sum(acc, axis=1, keepdims=True)
    square = (BATCH, BATCH)
    same = lax.broadcasted_iota(jnp.int32, square, 0) == lax.broadcasted_iota(jnp.int32, square, 1)
    labels = jnp.sum(
        jnp.where(same, jnp.broadcast_to(labels_ref[...], square), 0.0), axis=1, keepdims=True
    )
    loss = jnp.maximum(logit, 0.0) + jnp.log1p(jnp.exp(-jnp.abs(logit))) - labels * logit
    loss_ref[...] = jnp.sum(
        jnp.where(same, jnp.broadcast_to(loss, square), 0.0), axis=0, keepdims=True
    )
    dlogit = jnp.broadcast_to(jax.nn.sigmoid(logit) - labels, (BATCH, WIDTH))
    for t in range(FIELDS):
        x_ref[t * BATCH : (t + 1) * BATCH] = (dlogit * head[t : t + 1]).astype(bf16).astype(f32)

    low = lax.broadcasted_iota(jnp.int32, (RANK, WIDTH), 0) >= NF - RANK
    for layer in reversed(range(layers)):
        summary, nhat, rstd_fm, z, gate = saved[layer]
        gain = gain_out_ref[layer : layer + 1]
        for at in range(0, rows, chunk):
            cut = slice(at, at + chunk)
            xhat = xhat_ref[layer, cut]
            dxhat = x_ref[cut] * gain
            mean_d = jnp.mean(dxhat, axis=1, keepdims=True)
            mean_p = jnp.mean(dxhat * xhat, axis=1, keepdims=True)
            t_ref[cut] = rstd_ref[layer, cut] * (dxhat - mean_d - xhat * mean_p)
        dmachine = jnp.concatenate(
            [t_ref[n * BATCH : (n + 1) * BATCH].astype(bf16) for n in range(NF)], axis=1
        )
        dhidden = dot(dmachine, mlp_out_ref[layer], ((1,), (1,))).astype(bf16).astype(f32)
        dz = (dhidden * gate * (1.0 + z * (1.0 - gate))).astype(bf16)
        dnormed = dot(dz, mlp_in_ref[layer], ((1,), (1,))).astype(bf16).astype(f32)
        dnhat = dnormed * gain_fm_ref[layer : layer + 1]
        mean_d = jnp.mean(dnhat, axis=1, keepdims=True)
        mean_p = jnp.mean(dnhat * nhat, axis=1, keepdims=True)
        dflat = rstd_fm * (dnhat - mean_d - nhat * mean_p)
        for q in range(FIELDS // BATCH):
            part = dflat[:, q * WIDTH : (q + 1) * WIDTH]
            for j in range(BATCH):
                at = (q * BATCH + j) * BATCH
                only = jnp.where(lane == j, part, 0.0)
                d_ref[at : at + BATCH] = slide(only, -j * RANK).astype(bf16)
        dpairs = d_ref[...]
        dsummary = dot(dpairs, xb_ref[layer], ((0,), (0,)))
        parts = []
        for e in range(BATCH):
            straight = example(t_ref, e)
            parts.append(
                jnp.concatenate(
                    [
                        dsummary[e * RANK : (e + 1) * RANK],
                        jnp.where(low, straight[RANK : 2 * RANK], 0.0),
                        straight[2 * RANK :],
                    ],
                    axis=0,
                ).astype(bf16)
            )
        dacross = dot(mix_ref[layer], jnp.concatenate(parts, axis=1), ((0,), (0,)))
        for e in range(BATCH):
            x_ref[pl.ds(e, FIELDS, stride=BATCH), :] = dacross[:, e * WIDTH : (e + 1) * WIDTH]
        for at in range(0, rows, chunk):
            cut = slice(at, at + chunk)
            dx = x_ref[cut] + t_ref[cut] + dot(d_ref[cut], summary, ((1,), (0,)))
            x_ref[cut] = dx.astype(bf16).astype(f32)

    for group in range(groups):
        for column in range(COLUMNS):
            for half, table in enumerate((column, COLUMNS + column // 2)):
                at = (group * tables + table) * BATCH
                back_ref[column, group, half] = x_ref[at : at + BATCH].astype(bf16)


def mix_of(proj, compress):
    layers = proj.shape[0]
    gap = jnp.zeros((layers, NF - RANK, FIELDS), proj.dtype)
    return jnp.concatenate([jnp.transpose(proj, (0, 2, 1)), gap, compress], axis=1)


def counts_kernel(where_ref, b0_ref, b1_ref, b2_ref, b3_ref, counts_ref, idx_ref):
    rows, examples = counts_ref.shape
    column, core = where_ref[0], where_ref[1]
    for hop, bags_ref in enumerate((b0_ref, b1_ref, b2_ref, b3_ref)):
        at = pl.multiple_of(((column + hop) & (COLUMNS - 1)) * 128, 128)
        coded = bags_ref[:8]
        side = ((coded >> 7) & 1) ^ core
        spot = (side << 10) | ((coded >> 8) << 7) | (coded & 127)
        idx_ref[:8, pl.ds(at, 128)] = jnp.where(coded < DEAD, spot, -1).astype(jnp.float32)
        coded = bags_ref[8:]
        side = ((coded >> 6) & 1) ^ core
        spot = (side << 9) | ((coded >> 8) << 6) | (coded & 63)
        mine = ((coded >> 7) & 1) == (column & 1)
        spot = jnp.where(mine & (coded < DEAD), spot, -1)
        idx_ref[8:, pl.ds(at, 128)] = spot.astype(jnp.float32)
    ids = [
        (lax.broadcasted_iota(jnp.int32, (16, 128), 0) + 16 * i)
        .astype(jnp.float32)
        .astype(jnp.bfloat16)
        for i in range(256 // 16)
    ]
    one = jnp.ones((16, 128), jnp.bfloat16)
    zero = jnp.zeros((16, 128), jnp.bfloat16)

    def per_window(window, carry):
        half = window // 8
        first = ((window - 8 * half) * 256).astype(jnp.float32)
        for run in range(examples // 128):
            cut = slice(run * 128, run * 128 + 128)
            slots = idx_ref[pl.ds(pl.multiple_of(half * 8, 8), 8), cut] - first
            keys = [
                jnp.broadcast_to(slots[b : b + 1], (16, 128)).astype(jnp.bfloat16) for b in range(8)
            ]
            for i in range(len(ids)):
                hits = [jnp.where(keys[b] == ids[i], one, zero) for b in range(8)]
                while len(hits) > 1:
                    hits = [hits[k] + hits[k + 1] for k in range(0, len(hits), 2)]
                at = pl.multiple_of(window * 256 + i * 16, 16)
                counts_ref[pl.ds(at, 16), cut] = hits[0]
        return carry

    lax.fori_loop(0, rows // 256, per_window, 0)


def spans(rows):
    share = rows // 6
    return ((0, 2 * share), (4 * share, share))


def pool_kernel(counts_ref, mine_ref, other_ref, pools_ref):
    rows, examples = counts_ref.shape
    shards = mine_ref.shape[0]
    for half, (first, share) in enumerate(spans(rows)):
        deep = share // shards
        start = half * 2 * deep
        total = None
        for side, ref in enumerate((mine_ref, other_ref)):
            at = first + side * share
            part = dot(
                counts_ref[at : at + share],
                ref[:, start : start + deep].reshape(share, WIDTH),
                ((0,), (0,)),
            )
            total = part if total is None else total + part
        pools_ref[:, half] = total.astype(jnp.bfloat16).reshape(examples // BATCH, BATCH, WIDTH)


def grads_kernel(side, counts_ref, moved_ref, out_ref):
    rows, examples = counts_ref.shape
    shards = out_ref.shape[0]
    for half, (first, share) in enumerate(spans(rows)):
        deep = share // shards
        start = half * 2 * deep
        at = first + side * share
        grads = moved_ref[:, half].reshape(examples, WIDTH)
        acc = dot(counts_ref[at : at + share], grads, ((1,), (0,))).astype(jnp.bfloat16)
        out_ref[:, start : start + deep] = acc.reshape(shards, deep, WIDTH)


def add_kernel(left_ref, right_ref, out_ref):
    for at in range(out_ref.shape[0]):
        total = left_ref[at].astype(jnp.float32) + right_ref[at].astype(jnp.float32)
        out_ref[at] = total.astype(jnp.bfloat16)


def swap(values, axes):
    return lax.all_to_all(values, axes, split_axis=0, concat_axis=0, tiled=True)


def call(kernel, out_shape, ins, args, scratch=(), limit=VMEM_LIMIT):
    vmem = pl.BlockSpec(memory_space=pltpu.VMEM)
    smem = pl.BlockSpec(memory_space=pltpu.SMEM)
    hbm = pl.BlockSpec(memory_space=pltpu.HBM)
    many = isinstance(out_shape, tuple)
    return pl.pallas_call(
        kernel,
        out_shape=out_shape,
        in_specs=[{"s": smem, "v": vmem, "h": hbm}[kind] for kind in ins],
        out_specs=(vmem,) * len(out_shape) if many else vmem,
        scratch_shapes=list(scratch),
        compiler_params=pltpu.CompilerParams(vmem_limit_bytes=limit),
    )(*args)


def per_device(
    table_rows, bag_rows, bag_lens, labels, proj, mlp_in, mlp_out, compress, gain_fm, gain_out, head
):
    f32, bf16 = jnp.float32, jnp.bfloat16
    shape = jax.ShapeDtypeStruct
    tables, rows_dev, width = table_rows.shape
    layers = proj.shape[0]
    rep = lax.axis_index(REP)
    sub = lax.axis_index(SUB)
    column, core = lax.axis_index("x"), lax.axis_index("core")
    shards, groups, reps, across = 8, 8, 8, [(0, 1), (1, 0)]
    share = rows_dev // 2
    examples = COLUMNS * groups * BATCH
    piece = shape((shards, share + share // 2, width), bf16)
    per_owner = shape((COLUMNS * groups, 2, BATCH, width), bf16)

    def of_table(table, first, count):
        return lax.dynamic_slice(table_rows, (table, first, 0), (1, count, width))[0]

    part = jnp.concatenate(
        [
            of_table(column, core * share, share),
            of_table(
                COLUMNS + column // 2, (column & 1) * share + core * (share // 2), share // 2
            ),
        ]
    )
    gathered = swap(jnp.broadcast_to(part, piece.shape), SUB)
    coded = call(
        pick_kernel,
        (shape((16, 128), jnp.int32),) * COLUMNS,
        "shh",
        (jnp.stack([sub, column]), jnp.transpose(bag_rows, (1, 2, 0)), jnp.transpose(bag_lens)),
        [
            pltpu.VMEM((tables, 8, bag_rows.shape[0]), jnp.int32),
            pltpu.VMEM((tables, bag_rows.shape[0]), jnp.int32),
            pltpu.VMEM((tables, 8, 128), jnp.int32),
            pltpu.SemaphoreType.DMA((2,)),
        ],
        DENSE_LIMIT,
    )
    bags = [coded[0]] + [
        lax.ppermute(coded[hop], "x", [((i + hop) % COLUMNS, i) for i in range(COLUMNS)])
        for hop in range(1, COLUMNS)
    ]
    counts = call(
        counts_kernel,
        shape((2 * 6 * rows_dev, examples), bf16),
        "svvvv",
        (jnp.stack([column, core]), *bags),
        [pltpu.VMEM((16, examples), f32)],
    )
    gathered, counts = lax.optimization_barrier((gathered, counts))
    other = lax.ppermute(gathered, "core", across)
    other, mix = lax.optimization_barrier((other, mix_of(proj, compress)))
    pools = call(pool_kernel, per_owner, "vvv", (counts, gathered, other))
    near = swap(pools, ("x",) + GRP).reshape(COLUMNS, groups, 2, BATCH, width)

    rows = FIELDS * BATCH
    losses, back = call(
        dense_kernel,
        (shape((1, BATCH), f32), shape(near.shape, bf16)),
        "h" * 8,
        (
            labels.reshape(1, BATCH),
            near,
            mix,
            gain_fm,
            mlp_in,
            mlp_out,
            gain_out,
            head,
        ),
        [
            pltpu.VMEM((rows, WIDTH), f32),
            pltpu.VMEM((rows, WIDTH), f32),
            pltpu.VMEM((layers, rows, WIDTH), f32),
            pltpu.VMEM((layers, rows, 1), f32),
            pltpu.VMEM((layers + 1, rows, WIDTH), bf16),
            pltpu.VMEM((rows, WIDTH), bf16),
            pltpu.VMEM(near.shape, bf16),
            pltpu.VMEM(mix.shape, bf16),
            pltpu.VMEM(gain_fm.shape, f32),
            pltpu.VMEM(mlp_in.shape, bf16),
            pltpu.VMEM(mlp_out.shape, bf16),
            pltpu.VMEM(gain_out.shape, f32),
            pltpu.VMEM(head.shape, bf16),
            pltpu.VMEM((1, BATCH), f32),
            pltpu.SemaphoreType.DMA((9,)),
        ],
        DENSE_LIMIT,
    )

    returned = swap(back.reshape(per_owner.shape), ("x",) + GRP)
    other = call(functools.partial(grads_kernel, 1), piece, "vv", (counts, returned))
    other = lax.ppermute(other, "core", across)
    mine = call(functools.partial(grads_kernel, 0), piece, "vv", (counts, returned))
    pieces = swap(call(add_kernel, piece, "vv", (mine, other)), SUB)
    own = jnp.sum(pieces.astype(f32), axis=0).astype(bf16)
    spread = swap(jnp.broadcast_to(own, (reps, *own.shape)), REP)
    row_grads = jnp.concatenate(
        [
            spread[:, :share].reshape(COLUMNS, rows_dev, width),
            spread[:, share:].reshape(COLUMNS // 2, rows_dev, width),
        ]
    )
    return (losses.reshape(BATCH), row_grads.astype(f32))


def solution(mesh):
    view = Mesh(
        mesh.devices.reshape(4, 2, 4, 2, 8), ("x", "core", "y", "zhi", "sub")
    )
    return jax.shard_map(
        per_device,
        mesh=view,
        in_specs=(
            P(GRP, SUB, None),
            P(REP, GRP, None),
            P(REP, GRP),
            P(REP + GRP + SUB),
            P(),
            P(),
            P(),
            P(),
            P(),
            P(),
            P(),
        ),
        out_specs=(P(REP + GRP + SUB), P(GRP, SUB, None)),
        check_vma=False,
    )
```

```python
import functools

import jax
import jax.numpy as jnp
from jax import lax
from jax.experimental import pallas as pl
from jax.experimental.pallas import tpu as pltpu
from jax.sharding import Mesh
from jax.sharding import PartitionSpec as P

REP = ("x", "core")
GRP = ("y", "zhi")
SUB = ("quad", "pair")
DEAD = 4095
COLUMNS = 4
FIELDS, BATCH, WIDTH, RANK, NF = 48, 16, 128, 8, 12
VMEM_LIMIT = 24 * 1024 * 1024
DENSE_LIMIT = 56 * 1024 * 1024


def pick_kernel(where_ref, rows_hbm, lens_hbm, *refs):
    outs, (rows_ref, lens_ref, kept_ref, sems) = refs[:COLUMNS], refs[COLUMNS:]
    fetches = [
        pltpu.make_async_copy(rows_hbm, rows_ref, sems.at[0]),
        pltpu.make_async_copy(lens_hbm, lens_ref, sems.at[1]),
    ]
    for fetch in fetches:
        fetch.start()
    for fetch in fetches:
        fetch.wait()
    bag = rows_ref.shape[1]
    slots = lax.broadcasted_iota(jnp.int32, (bag, 128), 0)
    lanes = lax.broadcasted_iota(jnp.int32, (bag, 128), 1)
    column, quad, pair = where_ref[0], where_ref[2], where_ref[3]
    for table in range(rows_ref.shape[0]):
        for group in range(2):
            kept = jnp.zeros((bag, 128), jnp.int32)
            for run in range(4):
                at = (group * 4 + run) * 128
                cut = slice(at, at + 128)
                coded = jnp.where(
                    slots < lens_ref[table : table + 1, cut], rows_ref[table, :, cut], DEAD
                )
                moved = pltpu.roll(coded, (run * 32 - quad * 32) & 127, 1)
                kept = jnp.where(lanes // 32 == run, moved, kept)
            kept_ref[table, :, group * 128 : group * 128 + 128] = kept
    for hop in range(COLUMNS):
        target = (column - hop) & (COLUMNS - 1)
        outs[hop][...] = kept_ref[jnp.where(pair == 0, target, COLUMNS + (target >> 1))]


def dot(a, b, dims):
    return lax.dot_general(a, b, (dims, ((), ())), preferred_element_type=jnp.float32)


def slide(values, shift):
    halves = []
    for half in range(2):
        part = values[half * 8 : half * 8 + 8]
        base = (shift + half * 64) % WIDTH
        if base + 7 * RANK >= WIDTH:
            part, base = pltpu.roll(part, base, 1), 0
        halves.append(pltpu.roll(part, base, 1, stride=RANK, stride_axis=0))
    return jnp.concatenate(halves, axis=0)


def dense_kernel(
    labels_hbm, near_hbm, mix_hbm, gain_fm_hbm, mlp_in_hbm, mlp_out_hbm, gain_out_hbm, head_hbm,
    loss_ref, back_ref,
    x_ref, t_ref, xhat_ref, rstd_ref, xb_ref, d_ref,
    near_ref, mix_ref, gain_fm_ref, mlp_in_ref, mlp_out_ref, gain_out_ref, head_ref, labels_ref, sems,
):
    f32, bf16 = jnp.float32, jnp.bfloat16
    layers = mix_ref.shape[0]
    rows = FIELDS * BATCH
    chunk = 128
    lane = lax.broadcasted_iota(jnp.int32, (BATCH, WIDTH), 1) // RANK
    pairs = (
        (near_hbm, near_ref),
        (mix_hbm, mix_ref),
        (gain_fm_hbm, gain_fm_ref),
        (mlp_in_hbm, mlp_in_ref),
        (mlp_out_hbm.at[0], mlp_out_ref.at[0]),
        (gain_out_hbm, gain_out_ref),
        (mlp_out_hbm.at[1], mlp_out_ref.at[1]),
        (head_hbm, head_ref),
        (labels_hbm, labels_ref),
    )
    fetches = [pltpu.make_async_copy(*pair, sems.at[i]) for i, pair in enumerate(pairs)]
    for fetch in fetches:
        fetch.start()

    fetches[0].wait()
    groups = near_ref.shape[1]
    tables = FIELDS // groups
    for group in range(groups):
        for table in range(tables):
            if table < COLUMNS:
                whole = near_ref[table, group, 0]
            else:
                first = 2 * (table - COLUMNS)
                whole = near_ref[first, group, 1].astype(f32) + near_ref[first + 1, group, 1].astype(f32)
            at = (group * tables + table) * BATCH
            xb_ref[0, at : at + BATCH] = whole.astype(bf16)
    x_ref[...] = xb_ref[0].astype(f32)

    def example(ref, e):
        return ref[pl.ds(e, FIELDS, stride=BATCH), :]

    saved = []
    for layer in range(layers):
        across = jnp.concatenate([example(x_ref, e).astype(bf16) for e in range(BATCH)], axis=1)
        if layer == 0:
            fetches[1].wait()
        mixed = dot(mix_ref[layer], across, ((1,), (0,)))
        for e in range(BATCH):
            t_ref[pl.ds(e, FIELDS, stride=BATCH), :] = mixed[:, e * WIDTH : (e + 1) * WIDTH]
        pieces = [mixed[:RANK, e * WIDTH : (e + 1) * WIDTH] for e in range(BATCH)]
        summary = jnp.concatenate(pieces, axis=0).astype(bf16)
        mirrored = jnp.concatenate(pieces[::-1], axis=0).astype(bf16)
        pairs = dot(xb_ref[layer], mirrored, ((1,), (1,)))
        flat = []
        for q in range(FIELDS // BATCH):
            acc = jnp.zeros((BATCH, WIDTH), f32)
            for j in range(BATCH):
                at = (q * BATCH + j) * BATCH
                moved = slide(pairs[at : at + BATCH], (j + 1) * RANK)
                acc = jnp.where(lane == j, moved, acc)
            flat.append(acc)
        flat = jnp.concatenate(flat, axis=1)
        center = jnp.mean(flat, axis=1, keepdims=True)
        flat = flat - center
        rstd_fm = lax.rsqrt(jnp.mean(flat * flat, axis=1, keepdims=True) + 1e-05)
        nhat = flat * rstd_fm
        if layer == 0:
            fetches[2].wait()
            fetches[3].wait()
        normed = (nhat * gain_fm_ref[layer : layer + 1]).astype(bf16)
        z = dot(normed, mlp_in_ref[layer], ((1,), (0,)))
        gate = jax.nn.sigmoid(z)
        hidden = (z * gate).astype(bf16)
        if layer == 0:
            fetches[4].wait()
            fetches[5].wait()
        if layer == 1:
            fetches[6].wait()
        machine = dot(hidden, mlp_out_ref[layer], ((1,), (0,)))
        for n in range(NF):
            t_ref[n * BATCH : (n + 1) * BATCH] = machine[:, n * WIDTH : (n + 1) * WIDTH]
        gain = gain_out_ref[layer : layer + 1]
        for at in range(0, rows, chunk):
            cut = slice(at, at + chunk)
            total = t_ref[cut] + x_ref[cut]
            total = total - jnp.mean(total, axis=1, keepdims=True)
            rstd = lax.rsqrt(jnp.mean(total * total, axis=1, keepdims=True) + 1e-05)
            xhat = total * rstd
            xhat_ref[layer, cut] = xhat
            rstd_ref[layer, cut] = rstd
            out = (xhat * gain).astype(bf16)
            xb_ref[layer + 1, cut] = out
            x_ref[cut] = out.astype(f32)
        saved.append((summary, nhat, rstd_fm, z, gate))

    acc = jnp.zeros((BATCH, WIDTH), f32)
    fetches[7].wait()
    fetches[8].wait()
    head = head_ref[...].astype(f32)
    for t in range(FIELDS):
        acc = acc + x_ref[t * BATCH : (t + 1) * BATCH] * head[t : t + 1]
    logit = jnp.sum(acc, axis=1, keepdims=True)
    square = (BATCH, BATCH)
    same = lax.broadcasted_iota(jnp.int32, square, 0) == lax.broadcasted_iota(jnp.int32, square, 1)
    labels = jnp.sum(
        jnp.where(same, jnp.broadcast_to(labels_ref[...], square), 0.0), axis=1, keepdims=True
    )
    loss = jnp.maximum(logit, 0.0) + jnp.log1p(jnp.exp(-jnp.abs(logit))) - labels * logit
    loss_ref[...] = jnp.sum(
        jnp.where(same, jnp.broadcast_to(loss, square), 0.0), axis=0, keepdims=True
    )
    dlogit = jnp.broadcast_to(jax.nn.sigmoid(logit) - labels, (BATCH, WIDTH))
    for t in range(FIELDS):
        x_ref[t * BATCH : (t + 1) * BATCH] = (dlogit * head[t : t + 1]).astype(bf16).astype(f32)

    low = lax.broadcasted_iota(jnp.int32, (RANK, WIDTH), 0) >= NF - RANK
    for layer in reversed(range(layers)):
        summary, nhat, rstd_fm, z, gate = saved[layer]
        gain = gain_out_ref[layer : layer + 1]
        for at in range(0, rows, chunk):
            cut = slice(at, at + chunk)
            xhat = xhat_ref[layer, cut]
            dxhat = x_ref[cut] * gain
            mean_d = jnp.mean(dxhat, axis=1, keepdims=True)
            mean_p = jnp.mean(dxhat * xhat, axis=1, keepdims=True)
            t_ref[cut] = rstd_ref[layer, cut] * (dxhat - mean_d - xhat * mean_p)
        dmachine = jnp.concatenate(
            [t_ref[n * BATCH : (n + 1) * BATCH].astype(bf16) for n in range(NF)], axis=1
        )
        dhidden = dot(dmachine, mlp_out_ref[layer], ((1,), (1,))).astype(bf16).astype(f32)
        dz = (dhidden * gate * (1.0 + z * (1.0 - gate))).astype(bf16)
        dnormed = dot(dz, mlp_in_ref[layer], ((1,), (1,))).astype(bf16).astype(f32)
        dnhat = dnormed * gain_fm_ref[layer : layer + 1]
        mean_d = jnp.mean(dnhat, axis=1, keepdims=True)
        mean_p = jnp.mean(dnhat * nhat, axis=1, keepdims=True)
        dflat = rstd_fm * (dnhat - mean_d - nhat * mean_p)
        for q in range(FIELDS // BATCH):
            part = dflat[:, q * WIDTH : (q + 1) * WIDTH]
            for j in range(BATCH):
                at = (q * BATCH + j) * BATCH
                only = jnp.where(lane == j, part, 0.0)
                d_ref[at : at + BATCH] = slide(only, -j * RANK).astype(bf16)
        dpairs = d_ref[...]
        dsummary = dot(dpairs, xb_ref[layer], ((0,), (0,)))
        parts = []
        for e in range(BATCH):
            straight = example(t_ref, e)
            parts.append(
                jnp.concatenate(
                    [
                        dsummary[e * RANK : (e + 1) * RANK],
                        jnp.where(low, straight[RANK : 2 * RANK], 0.0),
                        straight[2 * RANK :],
                    ],
                    axis=0,
                ).astype(bf16)
            )
        dacross = dot(mix_ref[layer], jnp.concatenate(parts, axis=1), ((0,), (0,)))
        for e in range(BATCH):
            x_ref[pl.ds(e, FIELDS, stride=BATCH), :] = dacross[:, e * WIDTH : (e + 1) * WIDTH]
        for at in range(0, rows, chunk):
            cut = slice(at, at + chunk)
            dx = x_ref[cut] + t_ref[cut] + dot(d_ref[cut], summary, ((1,), (0,)))
            x_ref[cut] = dx.astype(bf16).astype(f32)

    for group in range(groups):
        for column in range(COLUMNS):
            for half, table in enumerate((column, COLUMNS + column // 2)):
                at = (group * tables + table) * BATCH
                back_ref[column, group, half] = x_ref[at : at + BATCH].astype(bf16)


def mix_of(proj, compress):
    layers = proj.shape[0]
    gap = jnp.zeros((layers, NF - RANK, FIELDS), proj.dtype)
    return jnp.concatenate([jnp.transpose(proj, (0, 2, 1)), gap, compress], axis=1)


def counts_kernel(where_ref, bags_ref, counts_ref, idx_ref):
    rows, examples = counts_ref.shape
    column, core, pair = where_ref[0], where_ref[1], where_ref[3]
    coded = bags_ref[...]
    top, low = (coded >> 7) & 1, (coded >> 6) & 1
    shard = (coded >> 8) << 7
    whole = ((top ^ core) << 10) | shard | (coded & 127)
    partial = jnp.where(top == (column & 1), ((low ^ core) << 10) | shard | (coded & 63), -1)
    spot = jnp.where(coded < DEAD, jnp.where(pair == 0, whole, partial), -1)
    idx_ref[...] = spot.astype(jnp.float32)
    ids = [
        (lax.broadcasted_iota(jnp.int32, (16, 128), 0) + 16 * i)
        .astype(jnp.float32)
        .astype(jnp.bfloat16)
        for i in range(256 // 16)
    ]
    one = jnp.ones((16, 128), jnp.bfloat16)
    zero = jnp.zeros((16, 128), jnp.bfloat16)

    def per_window(window, carry):
        first = (window * 256).astype(jnp.float32)
        for run in range(examples // 128):
            cut = slice(run * 128, run * 128 + 128)
            slots = idx_ref[:, cut] - first
            keys = [
                jnp.broadcast_to(slots[b : b + 1], (16, 128)).astype(jnp.bfloat16) for b in range(8)
            ]
            for i in range(len(ids)):
                hits = [jnp.where(keys[b] == ids[i], one, zero) for b in range(8)]
                while len(hits) > 1:
                    hits = [hits[k] + hits[k + 1] for k in range(0, len(hits), 2)]
                at = pl.multiple_of(window * 256 + i * 16, 16)
                counts_ref[pl.ds(at, 16), cut] = hits[0]
        return carry

    lax.fori_loop(0, rows // 256, per_window, 0)


def pool_kernel(where_ref, c0_ref, c1_ref, c2_ref, c3_ref, mine_ref, other_ref, pools_ref):
    column = where_ref[0]
    for hop, counts_ref in enumerate((c0_ref, c1_ref, c2_ref, c3_ref)):
        rows, examples = counts_ref.shape
        share = rows // 2
        total = dot(counts_ref[:share], mine_ref[...].reshape(share, WIDTH), ((0,), (0,)))
        total += dot(counts_ref[share:], other_ref[...].reshape(share, WIDTH), ((0,), (0,)))
        owners = examples // BATCH
        at = ((column + hop) & (COLUMNS - 1)) * owners
        pools_ref[pl.ds(at, owners)] = total.astype(jnp.bfloat16).reshape(owners, BATCH, WIDTH)


def grads_kernel(side, where_ref, c0_ref, c1_ref, c2_ref, c3_ref, moved_ref, out_ref):
    column = where_ref[0]
    total = None
    for hop, counts_ref in enumerate((c0_ref, c1_ref, c2_ref, c3_ref)):
        rows, examples = counts_ref.shape
        share = rows // 2
        owners = examples // BATCH
        at = ((column + hop) & (COLUMNS - 1)) * owners
        grads = moved_ref[pl.ds(at, owners)].reshape(examples, WIDTH)
        part = dot(counts_ref[side * share : side * share + share], grads, ((1,), (0,)))
        total = part if total is None else total + part
    out_ref[...] = total.astype(jnp.bfloat16).reshape(out_ref.shape)


def add_kernel(left_ref, right_ref, out_ref):
    for at in range(out_ref.shape[0]):
        total = left_ref[at].astype(jnp.float32) + right_ref[at].astype(jnp.float32)
        out_ref[at] = total.astype(jnp.bfloat16)


def swap(values, axes):
    return lax.all_to_all(values, axes, split_axis=0, concat_axis=0, tiled=True)


def call(kernel, out_shape, ins, args, scratch=(), limit=VMEM_LIMIT):
    vmem = pl.BlockSpec(memory_space=pltpu.VMEM)
    smem = pl.BlockSpec(memory_space=pltpu.SMEM)
    hbm = pl.BlockSpec(memory_space=pltpu.HBM)
    many = isinstance(out_shape, tuple)
    return pl.pallas_call(
        kernel,
        out_shape=out_shape,
        in_specs=[{"s": smem, "v": vmem, "h": hbm}[kind] for kind in ins],
        out_specs=(vmem,) * len(out_shape) if many else vmem,
        scratch_shapes=list(scratch),
        compiler_params=pltpu.CompilerParams(vmem_limit_bytes=limit),
    )(*args)


def per_device(
    table_rows, bag_rows, bag_lens, labels, proj, mlp_in, mlp_out, compress, gain_fm, gain_out, head
):
    f32, bf16 = jnp.float32, jnp.bfloat16
    shape = jax.ShapeDtypeStruct
    tables, rows_dev, width = table_rows.shape
    layers = proj.shape[0]
    column, core, quad, pair = (lax.axis_index(name) for name in ("x", "core") + SUB)
    where = jnp.stack([column, core, quad, pair])
    quads, pairs, groups, reps, across = 4, 2, 8, 8, [(0, 1), (1, 0)]
    share = rows_dev // 2
    owners = groups * pairs
    piece = shape((quads * pairs, share, width), bf16)
    per_owner = shape((COLUMNS * owners, BATCH, width), bf16)
    exchange = ("x",) + GRP + ("pair",)

    def of_table(table, first, count):
        return lax.dynamic_slice(table_rows, (table, first, 0), (1, count, width))

    whole = of_table(column, core * share, share)
    half = of_table(
        COLUMNS + column // 2, (column & 1) * share + core * (share // 2), share // 2
    )
    both = jnp.concatenate([whole, jnp.pad(half, ((0, 0), (0, share // 2), (0, 0)))])
    gathered = swap(
        jnp.broadcast_to(both, (quads, *both.shape)).reshape(piece.shape), SUB
    )
    coded = call(
        pick_kernel,
        (shape((8, owners * BATCH), jnp.int32),) * COLUMNS,
        "shh",
        (where, jnp.transpose(bag_rows, (1, 2, 0)), jnp.transpose(bag_lens)),
        [
            pltpu.VMEM((tables, 8, bag_rows.shape[0]), jnp.int32),
            pltpu.VMEM((tables, bag_rows.shape[0]), jnp.int32),
            pltpu.VMEM((tables, 8, owners * BATCH), jnp.int32),
            pltpu.SemaphoreType.DMA((2,)),
        ],
        DENSE_LIMIT,
    )
    bags = [coded[0]] + [
        lax.ppermute(coded[hop], "x", [((i + hop) % COLUMNS, i) for i in range(COLUMNS)])
        for hop in range(1, COLUMNS)
    ]
    counts = [
        call(
            counts_kernel,
            shape((8 * rows_dev, owners * BATCH), bf16),
            "sv",
            (where, bag),
            [pltpu.VMEM((8, owners * BATCH), f32)],
        )
        for bag in bags
    ]
    gathered, *counts = lax.optimization_barrier((gathered, *counts))
    other = lax.ppermute(gathered, "core", across)
    other, mix = lax.optimization_barrier((other, mix_of(proj, compress)))
    pools = call(pool_kernel, per_owner, "svvvvvv", (where, *counts, gathered, other))
    near = swap(pools, exchange).reshape(COLUMNS, groups, pairs, BATCH, width)

    rows = FIELDS * BATCH
    losses, back = call(
        dense_kernel,
        (shape((1, BATCH), f32), shape(near.shape, bf16)),
        "h" * 8,
        (
            labels.reshape(1, BATCH),
            near,
            mix,
            gain_fm,
            mlp_in,
            mlp_out,
            gain_out,
            head,
        ),
        [
            pltpu.VMEM((rows, WIDTH), f32),
            pltpu.VMEM((rows, WIDTH), f32),
            pltpu.VMEM((layers, rows, WIDTH), f32),
            pltpu.VMEM((layers, rows, 1), f32),
            pltpu.VMEM((layers + 1, rows, WIDTH), bf16),
            pltpu.VMEM((rows, WIDTH), bf16),
            pltpu.VMEM(near.shape, bf16),
            pltpu.VMEM(mix.shape, bf16),
            pltpu.VMEM(gain_fm.shape, f32),
            pltpu.VMEM(mlp_in.shape, bf16),
            pltpu.VMEM(mlp_out.shape, bf16),
            pltpu.VMEM(gain_out.shape, f32),
            pltpu.VMEM(head.shape, bf16),
            pltpu.VMEM((1, BATCH), f32),
            pltpu.SemaphoreType.DMA((9,)),
        ],
        DENSE_LIMIT,
    )

    returned = swap(back.reshape(per_owner.shape), exchange)
    operands = (where, *counts, returned)
    other = call(functools.partial(grads_kernel, 1), piece, "svvvvv", operands)
    other = lax.ppermute(other, "core", across)
    mine = call(functools.partial(grads_kernel, 0), piece, "svvvvv", operands)
    pieces = swap(call(add_kernel, piece, "vv", (mine, other)), SUB)
    whole, half = jnp.sum(
        pieces.reshape(quads, pairs, share, width).astype(f32), axis=0
    ).astype(bf16)
    own = jnp.concatenate([whole, half[: share // 2]])
    spread = swap(jnp.broadcast_to(own, (reps, *own.shape)), REP)
    row_grads = jnp.concatenate(
        [
            spread[:, :share].reshape(COLUMNS, rows_dev, width),
            spread[:, share:].reshape(COLUMNS // 2, rows_dev, width),
        ]
    )
    return (losses.reshape(BATCH), row_grads.astype(f32))


def solution(mesh):
    view = Mesh(
        mesh.devices.reshape(4, 2, 4, 2, 4, 2), ("x", "core", "y", "zhi", "quad", "pair")
    )
    return jax.shard_map(
        per_device,
        mesh=view,
        in_specs=(
            P(GRP, SUB, None),
            P(REP, GRP, None),
            P(REP, GRP),
            P(REP + GRP + SUB),
            P(),
            P(),
            P(),
            P(),
            P(),
            P(),
            P(),
        ),
        out_specs=(P(REP + GRP + SUB), P(GRP, SUB, None)),
        check_vma=False,
    )
```

```python
import functools

import jax
import jax.numpy as jnp
from jax import lax
from jax.experimental import pallas as pl
from jax.experimental.pallas import tpu as pltpu
from jax.sharding import Mesh
from jax.sharding import PartitionSpec as P

REP = ("x", "core")
GRP = ("y", "zhi")
SUB = ("quad", "pair")
DEAD = 4095
COLUMNS = 4
FIELDS, BATCH, WIDTH, RANK, NF = 48, 16, 128, 8, 12
VMEM_LIMIT = 20 * 1024 * 1024
DENSE_LIMIT = 24 * 1024 * 1024


def pick_kernel(rows_hbm, lens_hbm, *refs):
    outs, (rows_ref, lens_ref, kept_ref, sems) = refs[:COLUMNS], refs[COLUMNS:]
    fetches = [
        pltpu.make_async_copy(rows_hbm, rows_ref, sems.at[0]),
        pltpu.make_async_copy(lens_hbm, lens_ref, sems.at[1]),
    ]
    for fetch in fetches:
        fetch.start()
    for fetch in fetches:
        fetch.wait()
    bag = rows_ref.shape[1]
    slots = lax.broadcasted_iota(jnp.int32, (bag, 128), 0)
    lanes = lax.broadcasted_iota(jnp.int32, (bag, 128), 1)
    column, quad, pair = (lax.axis_index(name) for name in ("x",) + SUB)
    for table in range(rows_ref.shape[0]):
        for group in range(2):
            kept = jnp.zeros((bag, 128), jnp.int32)
            for run in range(4):
                at = (group * 4 + run) * 128
                cut = slice(at, at + 128)
                coded = jnp.where(
                    slots < lens_ref[table : table + 1, cut], rows_ref[table, :, cut], DEAD
                )
                moved = pltpu.roll(coded, (run * 32 - quad * 32) & 127, 1)
                kept = jnp.where(lanes // 32 == run, moved, kept)
            kept_ref[table, :, group * 128 : group * 128 + 128] = kept
    for hop in range(COLUMNS):
        target = (column - hop) & (COLUMNS - 1)
        outs[hop][...] = kept_ref[jnp.where(pair == 0, target, COLUMNS + (target >> 1))]


def dot(a, b, dims):
    return lax.dot_general(a, b, (dims, ((), ())), preferred_element_type=jnp.float32)


def slide(values, shift):
    halves = []
    for half in range(2):
        part = values[half * 8 : half * 8 + 8]
        base = (shift + half * 64) % WIDTH
        if base + 7 * RANK >= WIDTH:
            part, base = pltpu.roll(part, base, 1), 0
        halves.append(pltpu.roll(part, base, 1, stride=RANK, stride_axis=0))
    return jnp.concatenate(halves, axis=0)


def dense_kernel(
    labels_hbm, near_hbm, mix_hbm, gain_fm_hbm, mlp_in_hbm, mlp_out_hbm, gain_out_hbm, head_hbm,
    loss_ref, back_ref,
    x_ref, t_ref, xhat_ref, rstd_ref, xb_ref, d_ref,
    near_ref, mix_ref, gain_fm_ref, mlp_in_ref, mlp_out_ref, gain_out_ref, head_ref, labels_ref, sems,
):
    f32, bf16 = jnp.float32, jnp.bfloat16
    layers = mix_ref.shape[0]
    rows = FIELDS * BATCH
    chunk = 128
    lane = lax.broadcasted_iota(jnp.int32, (BATCH, WIDTH), 1) // RANK
    pairs = (
        (near_hbm, near_ref),
        (mix_hbm, mix_ref),
        (gain_fm_hbm, gain_fm_ref),
        (mlp_in_hbm, mlp_in_ref),
        (mlp_out_hbm.at[0], mlp_out_ref.at[0]),
        (gain_out_hbm, gain_out_ref),
        (mlp_out_hbm.at[1], mlp_out_ref.at[1]),
        (head_hbm, head_ref),
        (labels_hbm, labels_ref),
    )
    fetches = [pltpu.make_async_copy(*pair, sems.at[i]) for i, pair in enumerate(pairs)]
    for fetch in fetches:
        fetch.start()

    fetches[0].wait()
    groups = near_ref.shape[1]
    tables = FIELDS // groups
    for group in range(groups):
        for table in range(tables):
            if table < COLUMNS:
                whole = near_ref[table, group, 0]
            else:
                first = 2 * (table - COLUMNS)
                whole = near_ref[first, group, 1].astype(f32) + near_ref[first + 1, group, 1].astype(f32)
            at = (group * tables + table) * BATCH
            xb_ref[0, at : at + BATCH] = whole.astype(bf16)
    x_ref[...] = xb_ref[0].astype(f32)

    def example(ref, e):
        return ref[pl.ds(e, FIELDS, stride=BATCH), :]

    saved = []
    for layer in range(layers):
        across = jnp.concatenate([example(x_ref, e).astype(bf16) for e in range(BATCH)], axis=1)
        if layer == 0:
            fetches[1].wait()
        mixed = dot(mix_ref[layer], across, ((1,), (0,)))
        for e in range(BATCH):
            t_ref[pl.ds(e, FIELDS, stride=BATCH), :] = mixed[:, e * WIDTH : (e + 1) * WIDTH]
        pieces = [mixed[:RANK, e * WIDTH : (e + 1) * WIDTH] for e in range(BATCH)]
        summary = jnp.concatenate(pieces, axis=0).astype(bf16)
        mirrored = jnp.concatenate(pieces[::-1], axis=0).astype(bf16)
        pairs = dot(xb_ref[layer], mirrored, ((1,), (1,)))
        flat = []
        for q in range(FIELDS // BATCH):
            acc = jnp.zeros((BATCH, WIDTH), f32)
            for j in range(BATCH):
                at = (q * BATCH + j) * BATCH
                moved = slide(pairs[at : at + BATCH], (j + 1) * RANK)
                acc = jnp.where(lane == j, moved, acc)
            flat.append(acc)
        flat = jnp.concatenate(flat, axis=1)
        center = jnp.mean(flat, axis=1, keepdims=True)
        flat = flat - center
        rstd_fm = lax.rsqrt(jnp.mean(flat * flat, axis=1, keepdims=True) + 1e-05)
        nhat = flat * rstd_fm
        if layer == 0:
            fetches[2].wait()
            fetches[3].wait()
        normed = (nhat * gain_fm_ref[layer : layer + 1]).astype(bf16)
        z = dot(normed, mlp_in_ref[layer], ((1,), (0,)))
        gate = jax.nn.sigmoid(z)
        hidden = (z * gate).astype(bf16)
        if layer == 0:
            fetches[4].wait()
            fetches[5].wait()
        if layer == 1:
            fetches[6].wait()
        machine = dot(hidden, mlp_out_ref[layer], ((1,), (0,)))
        for n in range(NF):
            t_ref[n * BATCH : (n + 1) * BATCH] = machine[:, n * WIDTH : (n + 1) * WIDTH]
        gain = gain_out_ref[layer : layer + 1]
        for at in range(0, rows, chunk):
            cut = slice(at, at + chunk)
            total = t_ref[cut] + x_ref[cut]
            total = total - jnp.mean(total, axis=1, keepdims=True)
            rstd = lax.rsqrt(jnp.mean(total * total, axis=1, keepdims=True) + 1e-05)
            xhat = total * rstd
            xhat_ref[layer, cut] = xhat
            rstd_ref[layer, cut] = rstd
            out = (xhat * gain).astype(bf16)
            xb_ref[layer + 1, cut] = out
            x_ref[cut] = out.astype(f32)
        saved.append((summary, nhat, rstd_fm, z, gate))

    acc = jnp.zeros((BATCH, WIDTH), f32)
    fetches[7].wait()
    fetches[8].wait()
    head = head_ref[...].astype(f32)
    for t in range(FIELDS):
        acc = acc + x_ref[t * BATCH : (t + 1) * BATCH] * head[t : t + 1]
    logit = jnp.sum(acc, axis=1, keepdims=True)
    square = (BATCH, BATCH)
    same = lax.broadcasted_iota(jnp.int32, square, 0) == lax.broadcasted_iota(jnp.int32, square, 1)
    labels = jnp.sum(
        jnp.where(same, jnp.broadcast_to(labels_ref[...], square), 0.0), axis=1, keepdims=True
    )
    loss = jnp.maximum(logit, 0.0) + jnp.log1p(jnp.exp(-jnp.abs(logit))) - labels * logit
    loss_ref[...] = jnp.sum(
        jnp.where(same, jnp.broadcast_to(loss, square), 0.0), axis=0, keepdims=True
    )
    dlogit = jnp.broadcast_to(jax.nn.sigmoid(logit) - labels, (BATCH, WIDTH))
    for t in range(FIELDS):
        x_ref[t * BATCH : (t + 1) * BATCH] = (dlogit * head[t : t + 1]).astype(bf16).astype(f32)

    low = lax.broadcasted_iota(jnp.int32, (RANK, WIDTH), 0) >= NF - RANK
    for layer in reversed(range(layers)):
        summary, nhat, rstd_fm, z, gate = saved[layer]
        gain = gain_out_ref[layer : layer + 1]
        for at in range(0, rows, chunk):
            cut = slice(at, at + chunk)
            xhat = xhat_ref[layer, cut]
            dxhat = x_ref[cut] * gain
            mean_d = jnp.mean(dxhat, axis=1, keepdims=True)
            mean_p = jnp.mean(dxhat * xhat, axis=1, keepdims=True)
            t_ref[cut] = rstd_ref[layer, cut] * (dxhat - mean_d - xhat * mean_p)
        dmachine = jnp.concatenate(
            [t_ref[n * BATCH : (n + 1) * BATCH].astype(bf16) for n in range(NF)], axis=1
        )
        dhidden = dot(dmachine, mlp_out_ref[layer], ((1,), (1,))).astype(bf16).astype(f32)
        dz = (dhidden * gate * (1.0 + z * (1.0 - gate))).astype(bf16)
        dnormed = dot(dz, mlp_in_ref[layer], ((1,), (1,))).astype(bf16).astype(f32)
        dnhat = dnormed * gain_fm_ref[layer : layer + 1]
        mean_d = jnp.mean(dnhat, axis=1, keepdims=True)
        mean_p = jnp.mean(dnhat * nhat, axis=1, keepdims=True)
        dflat = rstd_fm * (dnhat - mean_d - nhat * mean_p)
        for q in range(FIELDS // BATCH):
            part = dflat[:, q * WIDTH : (q + 1) * WIDTH]
            for j in range(BATCH):
                at = (q * BATCH + j) * BATCH
                only = jnp.where(lane == j, part, 0.0)
                d_ref[at : at + BATCH] = slide(only, -j * RANK).astype(bf16)
        dpairs = d_ref[...]
        dsummary = dot(dpairs, xb_ref[layer], ((0,), (0,)))
        parts = []
        for e in range(BATCH):
            straight = example(t_ref, e)
            parts.append(
                jnp.concatenate(
                    [
                        dsummary[e * RANK : (e + 1) * RANK],
                        jnp.where(low, straight[RANK : 2 * RANK], 0.0),
                        straight[2 * RANK :],
                    ],
                    axis=0,
                ).astype(bf16)
            )
        dacross = dot(mix_ref[layer], jnp.concatenate(parts, axis=1), ((0,), (0,)))
        for e in range(BATCH):
            x_ref[pl.ds(e, FIELDS, stride=BATCH), :] = dacross[:, e * WIDTH : (e + 1) * WIDTH]
        for at in range(0, rows, chunk):
            cut = slice(at, at + chunk)
            dx = x_ref[cut] + t_ref[cut] + dot(d_ref[cut], summary, ((1,), (0,)))
            x_ref[cut] = dx.astype(bf16).astype(f32)

    for group in range(groups):
        for column in range(COLUMNS):
            for half, table in enumerate((column, COLUMNS + column // 2)):
                at = (group * tables + table) * BATCH
                back_ref[column, group, half] = x_ref[at : at + BATCH].astype(bf16)


def mix_of(proj, compress):
    layers = proj.shape[0]
    gap = jnp.zeros((layers, NF - RANK, FIELDS), proj.dtype)
    return jnp.concatenate([jnp.transpose(proj, (0, 2, 1)), gap, compress], axis=1)


def counts_kernel(*refs):
    bags_refs, (counts_ref, idx_ref) = refs[:-2], refs[-2:]
    rows, examples = counts_ref.shape
    column, core, pair = (lax.axis_index(name) for name in ("x", "core", "pair"))
    for hop, bags_ref in enumerate(bags_refs):
        coded = bags_ref[...]
        top, low = (coded >> 7) & 1, (coded >> 6) & 1
        shard = (coded >> 8) << 7
        whole = ((top ^ core) << 10) | shard | (coded & 127)
        partial = jnp.where(top == (column & 1), ((low ^ core) << 10) | shard | (coded & 63), -1)
        spot = jnp.where(coded < DEAD, jnp.where(pair == 0, whole, partial), -1)
        each = coded.shape[1]
        idx_ref[:, hop * each : hop * each + each] = spot.astype(jnp.float32)
    ids = [
        (lax.broadcasted_iota(jnp.int32, (16, 128), 0) + 16 * i)
        .astype(jnp.float32)
        .astype(jnp.bfloat16)
        for i in range(256 // 16)
    ]
    one = jnp.ones((16, 128), jnp.bfloat16)
    zero = jnp.zeros((16, 128), jnp.bfloat16)

    def per_window(window, carry):
        first = (window * 256).astype(jnp.float32)
        for run in range(examples // 128):
            cut = slice(run * 128, run * 128 + 128)
            slots = idx_ref[:, cut] - first
            keys = [
                jnp.broadcast_to(slots[b : b + 1], (16, 128)).astype(jnp.bfloat16) for b in range(8)
            ]
            for i in range(len(ids)):
                hits = [jnp.where(keys[b] == ids[i], one, zero) for b in range(8)]
                while len(hits) > 1:
                    hits = [hits[k] + hits[k + 1] for k in range(0, len(hits), 2)]
                at = pl.multiple_of(window * 256 + i * 16, 16)
                counts_ref[pl.ds(at, 16), cut] = hits[0]
        return carry

    lax.fori_loop(0, rows // 256, per_window, 0)


def by_column(first_ref, last_ref, owned):
    each = last_ref.shape[1]
    column = lax.axis_index("x")
    for hop in range(COLUMNS):
        ref, at = (first_ref, hop * each) if hop < COLUMNS - 1 else (last_ref, 0)
        yield ref, slice(at, at + each), pl.ds(((column + hop) & (COLUMNS - 1)) * owned, owned)


def pool_kernel(first_ref, last_ref, mine_ref, other_ref, pools_ref):
    share = first_ref.shape[0] // 2
    owned = pools_ref.shape[0] // COLUMNS
    for ref, cut, owners in by_column(first_ref, last_ref, owned):
        total = dot(ref[:share, cut], mine_ref[...].reshape(share, WIDTH), ((0,), (0,)))
        total += dot(ref[share:, cut], other_ref[...].reshape(share, WIDTH), ((0,), (0,)))
        pools_ref[owners] = total.astype(jnp.bfloat16).reshape(owned, BATCH, WIDTH)


def grads_kernel(side, first_ref, last_ref, moved_ref, out_ref):
    share = first_ref.shape[0] // 2
    owned = moved_ref.shape[0] // COLUMNS
    total = jnp.zeros((share, WIDTH), jnp.float32)
    for ref, cut, owners in by_column(first_ref, last_ref, owned):
        grads = moved_ref[owners].reshape(owned * BATCH, WIDTH)
        total += dot(ref[side * share : side * share + share, cut], grads, ((1,), (0,)))
    out_ref[...] = total.astype(jnp.bfloat16).reshape(out_ref.shape)


def add_kernel(left_ref, right_ref, out_ref):
    for at in range(out_ref.shape[0]):
        total = left_ref[at].astype(jnp.float32) + right_ref[at].astype(jnp.float32)
        out_ref[at] = total.astype(jnp.bfloat16)


def swap(values, axes):
    return lax.all_to_all(values, axes, split_axis=0, concat_axis=0, tiled=True)


def call(kernel, out_shape, ins, args, scratch=(), limit=VMEM_LIMIT):
    vmem = pl.BlockSpec(memory_space=pltpu.VMEM)
    smem = pl.BlockSpec(memory_space=pltpu.SMEM)
    hbm = pl.BlockSpec(memory_space=pltpu.HBM)
    many = isinstance(out_shape, tuple)
    return pl.pallas_call(
        kernel,
        out_shape=out_shape,
        in_specs=[{"s": smem, "v": vmem, "h": hbm}[kind] for kind in ins],
        out_specs=(vmem,) * len(out_shape) if many else vmem,
        scratch_shapes=list(scratch),
        compiler_params=pltpu.CompilerParams(vmem_limit_bytes=limit),
    )(*args)


def per_device(
    table_rows, bag_rows, bag_lens, labels, proj, mlp_in, mlp_out, compress, gain_fm, gain_out, head
):
    f32, bf16 = jnp.float32, jnp.bfloat16
    shape = jax.ShapeDtypeStruct
    tables, rows_dev, width = table_rows.shape
    layers = proj.shape[0]
    column, core = lax.axis_index("x"), lax.axis_index("core")
    quads, pairs, groups, reps, across = 4, 2, 8, 8, [(0, 1), (1, 0)]
    share = rows_dev // 2
    owners = groups * pairs
    piece = shape((quads * pairs, share, width), bf16)
    per_owner = shape((COLUMNS * owners, BATCH, width), bf16)
    exchange = ("x",) + GRP + ("pair",)

    def of_table(table, first, count):
        return lax.dynamic_slice(table_rows, (table, first, 0), (1, count, width))

    whole = of_table(column, core * share, share)
    half = of_table(
        COLUMNS + column // 2, (column & 1) * share + core * (share // 2), share // 2
    )
    both = jnp.concatenate([whole, jnp.pad(half, ((0, 0), (0, share // 2), (0, 0)))])
    gathered = swap(
        jnp.broadcast_to(both, (quads, *both.shape)).reshape(piece.shape), SUB
    )
    coded = call(
        pick_kernel,
        (shape((8, owners * BATCH), jnp.int32),) * COLUMNS,
        "hh",
        (jnp.transpose(bag_rows, (1, 2, 0)), jnp.transpose(bag_lens)),
        [
            pltpu.VMEM((tables, 8, bag_rows.shape[0]), jnp.int32),
            pltpu.VMEM((tables, bag_rows.shape[0]), jnp.int32),
            pltpu.VMEM((tables, 8, owners * BATCH), jnp.int32),
            pltpu.SemaphoreType.DMA((2,)),
        ],
        DENSE_LIMIT,
    )
    bags = [coded[0]] + [
        lax.ppermute(coded[hop], "x", [((i + hop) % COLUMNS, i) for i in range(COLUMNS)])
        for hop in range(1, COLUMNS)
    ]
    each = owners * BATCH

    def count(bags):
        examples = len(bags) * each
        return call(
            counts_kernel,
            shape((8 * rows_dev, examples), bf16),
            "v" * len(bags),
            bags,
            [pltpu.VMEM((8, examples), f32)],
        )

    first = count(bags[:-1])
    gathered, first, late = lax.optimization_barrier((gathered, first, bags[-1]))
    other = lax.ppermute(gathered, "core", across)
    last = count([late])
    other, last, mix = lax.optimization_barrier((other, last, mix_of(proj, compress)))
    pools = call(pool_kernel, per_owner, "vvvv", (first, last, gathered, other))
    near = swap(pools, exchange).reshape(COLUMNS, groups, pairs, BATCH, width)

    rows = FIELDS * BATCH
    losses, back = call(
        dense_kernel,
        (shape((1, BATCH), f32), shape(near.shape, bf16)),
        "h" * 8,
        (
            labels.reshape(1, BATCH),
            near,
            mix,
            gain_fm,
            mlp_in,
            mlp_out,
            gain_out,
            head,
        ),
        [
            pltpu.VMEM((rows, WIDTH), f32),
            pltpu.VMEM((rows, WIDTH), f32),
            pltpu.VMEM((layers, rows, WIDTH), f32),
            pltpu.VMEM((layers, rows, 1), f32),
            pltpu.VMEM((layers + 1, rows, WIDTH), bf16),
            pltpu.VMEM((rows, WIDTH), bf16),
            pltpu.VMEM(near.shape, bf16),
            pltpu.VMEM(mix.shape, bf16),
            pltpu.VMEM(gain_fm.shape, f32),
            pltpu.VMEM(mlp_in.shape, bf16),
            pltpu.VMEM(mlp_out.shape, bf16),
            pltpu.VMEM(gain_out.shape, f32),
            pltpu.VMEM(head.shape, bf16),
            pltpu.VMEM((1, BATCH), f32),
            pltpu.SemaphoreType.DMA((9,)),
        ],
        DENSE_LIMIT,
    )

    returned = swap(back.reshape(per_owner.shape), exchange)
    operands = (first, last, returned)
    other = call(functools.partial(grads_kernel, 1), piece, "vvv", operands)
    other = lax.ppermute(other, "core", across)
    mine = call(functools.partial(grads_kernel, 0), piece, "vvv", operands)
    pieces = swap(call(add_kernel, piece, "vv", (mine, other)), SUB)
    whole, half = jnp.sum(
        pieces.reshape(quads, pairs, share, width).astype(f32), axis=0
    ).astype(bf16)
    own = jnp.concatenate([whole, half[: share // 2]])
    spread = swap(jnp.broadcast_to(own, (reps, *own.shape)), REP)
    row_grads = jnp.concatenate(
        [
            spread[:, :share].reshape(COLUMNS, rows_dev, width),
            spread[:, share:].reshape(COLUMNS // 2, rows_dev, width),
        ]
    )
    return (losses.reshape(BATCH), row_grads.astype(f32))


def solution(mesh):
    view = Mesh(
        mesh.devices.reshape(4, 2, 4, 2, 4, 2), ("x", "core", "y", "zhi", "quad", "pair")
    )
    return jax.shard_map(
        per_device,
        mesh=view,
        in_specs=(
            P(GRP, SUB, None),
            P(REP, GRP, None),
            P(REP, GRP),
            P(REP + GRP + SUB),
            P(),
            P(),
            P(),
            P(),
            P(),
            P(),
            P(),
        ),
        out_specs=(P(REP + GRP + SUB), P(GRP, SUB, None)),
        check_vma=False,
    )
```

```python
import functools

import jax
import jax.numpy as jnp
from jax import lax
from jax.experimental import pallas as pl
from jax.experimental.pallas import tpu as pltpu
from jax.sharding import Mesh
from jax.sharding import PartitionSpec as P

REP = ("x", "core")
GRP = ("y", "zhi")
SUB = ("quad", "pair")
DEAD = 4095
COLUMNS = 4
FIELDS, BATCH, WIDTH, RANK, NF = 48, 16, 128, 8, 12
VMEM_LIMIT = 20 * 1024 * 1024


def pick_kernel(rows_hbm, lens_hbm, *refs):
    outs, (rows_ref, lens_ref, kept_ref, sems) = refs[:COLUMNS], refs[COLUMNS:]
    fetches = [
        pltpu.make_async_copy(rows_hbm, rows_ref, sems.at[0]),
        pltpu.make_async_copy(lens_hbm, lens_ref, sems.at[1]),
    ]
    for fetch in fetches:
        fetch.start()
    for fetch in fetches:
        fetch.wait()
    bag = rows_ref.shape[1]
    slots = lax.broadcasted_iota(jnp.int32, (bag, 128), 0)
    lanes = lax.broadcasted_iota(jnp.int32, (bag, 128), 1)
    column, quad, pair = (lax.axis_index(name) for name in ("x",) + SUB)
    for table in range(rows_ref.shape[0]):
        for group in range(2):
            kept = jnp.zeros((bag, 128), jnp.int32)
            for run in range(4):
                at = (group * 4 + run) * 128
                cut = slice(at, at + 128)
                coded = jnp.where(
                    slots < lens_ref[table : table + 1, cut], rows_ref[table, :, cut], DEAD
                )
                moved = pltpu.roll(coded, (run * 32 - quad * 32) & 127, 1)
                kept = jnp.where(lanes // 32 == run, moved, kept)
            kept_ref[table, :, group * 128 : group * 128 + 128] = kept
    for hop in range(COLUMNS):
        target = (column - hop) & (COLUMNS - 1)
        outs[hop][...] = kept_ref[jnp.where(pair == 0, target, COLUMNS + (target >> 1))]


def dot(a, b, dims):
    return lax.dot_general(a, b, (dims, ((), ())), preferred_element_type=jnp.float32)


def slide(values, shift):
    halves = []
    for half in range(2):
        part = values[half * 8 : half * 8 + 8]
        base = (shift + half * 64) % WIDTH
        if base + 7 * RANK >= WIDTH:
            part, base = pltpu.roll(part, base, 1), 0
        halves.append(pltpu.roll(part, base, 1, stride=RANK, stride_axis=0))
    return jnp.concatenate(halves, axis=0)


def dense_kernel(
    labels_ref, near_ref, mix_ref, gain_fm_ref, mlp_in_ref, mlp_out_ref, gain_out_ref, head_ref,
    loss_ref, back_ref,
    x_ref, t_ref, xhat_ref, rstd_ref, xb_ref, d_ref,
):
    f32, bf16 = jnp.float32, jnp.bfloat16
    layers = mix_ref.shape[0]
    rows = FIELDS * BATCH
    chunk = 128
    lane = lax.broadcasted_iota(jnp.int32, (BATCH, WIDTH), 1) // RANK
    zs, ys = near_ref.shape[:2]
    groups = ys * zs
    tables = FIELDS // groups
    for group in range(groups):
        for table in range(tables):
            if table < COLUMNS:
                whole = near_ref[group % zs, group // zs, table, 0]
            else:
                first = 2 * (table - COLUMNS)
                halves = near_ref.at[group % zs, group // zs]
                whole = halves[first, 1].astype(f32) + halves[first + 1, 1].astype(f32)
            at = (group * tables + table) * BATCH
            xb_ref[0, at : at + BATCH] = whole.astype(bf16)
    x_ref[...] = xb_ref[0].astype(f32)

    def example(ref, e):
        return ref[pl.ds(e, FIELDS, stride=BATCH), :]

    saved = []
    for layer in range(layers):
        across = jnp.concatenate([example(x_ref, e).astype(bf16) for e in range(BATCH)], axis=1)
        mixed = dot(mix_ref[layer], across, ((1,), (0,)))
        for e in range(BATCH):
            t_ref[pl.ds(e, FIELDS, stride=BATCH), :] = mixed[:, e * WIDTH : (e + 1) * WIDTH]
        pieces = [mixed[:RANK, e * WIDTH : (e + 1) * WIDTH] for e in range(BATCH)]
        summary = jnp.concatenate(pieces, axis=0).astype(bf16)
        mirrored = jnp.concatenate(pieces[::-1], axis=0).astype(bf16)
        pairs = dot(xb_ref[layer], mirrored, ((1,), (1,)))
        flat = []
        for q in range(FIELDS // BATCH):
            acc = jnp.zeros((BATCH, WIDTH), f32)
            for j in range(BATCH):
                at = (q * BATCH + j) * BATCH
                moved = slide(pairs[at : at + BATCH], (j + 1) * RANK)
                acc = jnp.where(lane == j, moved, acc)
            flat.append(acc)
        flat = jnp.concatenate(flat, axis=1)
        center = jnp.mean(flat, axis=1, keepdims=True)
        flat = flat - center
        rstd_fm = lax.rsqrt(jnp.mean(flat * flat, axis=1, keepdims=True) + 1e-05)
        nhat = flat * rstd_fm
        normed = (nhat * gain_fm_ref[layer : layer + 1]).astype(bf16)
        z = dot(normed, mlp_in_ref[layer], ((1,), (0,)))
        gate = jax.nn.sigmoid(z)
        hidden = (z * gate).astype(bf16)
        machine = dot(hidden, mlp_out_ref[layer], ((1,), (0,)))
        for n in range(NF):
            t_ref[n * BATCH : (n + 1) * BATCH] = machine[:, n * WIDTH : (n + 1) * WIDTH]
        gain = gain_out_ref[layer : layer + 1]
        for at in range(0, rows, chunk):
            cut = slice(at, at + chunk)
            total = t_ref[cut] + x_ref[cut]
            total = total - jnp.mean(total, axis=1, keepdims=True)
            rstd = lax.rsqrt(jnp.mean(total * total, axis=1, keepdims=True) + 1e-05)
            xhat = total * rstd
            xhat_ref[layer, cut] = xhat
            rstd_ref[layer, cut] = rstd
            out = (xhat * gain).astype(bf16)
            xb_ref[layer + 1, cut] = out
            x_ref[cut] = out.astype(f32)
        saved.append((summary, nhat, rstd_fm, z, gate))

    acc = jnp.zeros((BATCH, WIDTH), f32)
    head = head_ref[...].astype(f32)
    for t in range(FIELDS):
        acc = acc + x_ref[t * BATCH : (t + 1) * BATCH] * head[t : t + 1]
    logit = jnp.sum(acc, axis=1, keepdims=True)
    square = (BATCH, BATCH)
    same = lax.broadcasted_iota(jnp.int32, square, 0) == lax.broadcasted_iota(jnp.int32, square, 1)
    labels = jnp.sum(
        jnp.where(same, jnp.broadcast_to(labels_ref[...], square), 0.0), axis=1, keepdims=True
    )
    loss = jnp.maximum(logit, 0.0) + jnp.log1p(jnp.exp(-jnp.abs(logit))) - labels * logit
    loss_ref[...] = jnp.sum(
        jnp.where(same, jnp.broadcast_to(loss, square), 0.0), axis=0, keepdims=True
    )
    dlogit = jnp.broadcast_to(jax.nn.sigmoid(logit) - labels, (BATCH, WIDTH))
    for t in range(FIELDS):
        x_ref[t * BATCH : (t + 1) * BATCH] = (dlogit * head[t : t + 1]).astype(bf16).astype(f32)

    low = lax.broadcasted_iota(jnp.int32, (RANK, WIDTH), 0) >= NF - RANK
    for layer in reversed(range(layers)):
        summary, nhat, rstd_fm, z, gate = saved[layer]
        gain = gain_out_ref[layer : layer + 1]
        for at in range(0, rows, chunk):
            cut = slice(at, at + chunk)
            xhat = xhat_ref[layer, cut]
            dxhat = x_ref[cut] * gain
            mean_d = jnp.mean(dxhat, axis=1, keepdims=True)
            mean_p = jnp.mean(dxhat * xhat, axis=1, keepdims=True)
            t_ref[cut] = rstd_ref[layer, cut] * (dxhat - mean_d - xhat * mean_p)
        dmachine = jnp.concatenate(
            [t_ref[n * BATCH : (n + 1) * BATCH].astype(bf16) for n in range(NF)], axis=1
        )
        dhidden = dot(dmachine, mlp_out_ref[layer], ((1,), (1,))).astype(bf16).astype(f32)
        dz = (dhidden * gate * (1.0 + z * (1.0 - gate))).astype(bf16)
        dnormed = dot(dz, mlp_in_ref[layer], ((1,), (1,))).astype(bf16).astype(f32)
        dnhat = dnormed * gain_fm_ref[layer : layer + 1]
        mean_d = jnp.mean(dnhat, axis=1, keepdims=True)
        mean_p = jnp.mean(dnhat * nhat, axis=1, keepdims=True)
        dflat = rstd_fm * (dnhat - mean_d - nhat * mean_p)
        for q in range(FIELDS // BATCH):
            part = dflat[:, q * WIDTH : (q + 1) * WIDTH]
            for j in range(BATCH):
                at = (q * BATCH + j) * BATCH
                only = jnp.where(lane == j, part, 0.0)
                d_ref[at : at + BATCH] = slide(only, -j * RANK).astype(bf16)
        dpairs = d_ref[...]
        dsummary = dot(dpairs, xb_ref[layer], ((0,), (0,)))
        parts = []
        for e in range(BATCH):
            straight = example(t_ref, e)
            parts.append(
                jnp.concatenate(
                    [
                        dsummary[e * RANK : (e + 1) * RANK],
                        jnp.where(low, straight[RANK : 2 * RANK], 0.0),
                        straight[2 * RANK :],
                    ],
                    axis=0,
                ).astype(bf16)
            )
        dacross = dot(mix_ref[layer], jnp.concatenate(parts, axis=1), ((0,), (0,)))
        for e in range(BATCH):
            x_ref[pl.ds(e, FIELDS, stride=BATCH), :] = dacross[:, e * WIDTH : (e + 1) * WIDTH]
        for at in range(0, rows, chunk):
            cut = slice(at, at + chunk)
            dx = x_ref[cut] + t_ref[cut] + dot(d_ref[cut], summary, ((1,), (0,)))
            x_ref[cut] = dx.astype(bf16).astype(f32)

    for group in range(groups):
        for column in range(COLUMNS):
            for half, table in enumerate((column, COLUMNS + column // 2)):
                at = (group * tables + table) * BATCH
                back_ref[group % zs, group // zs, column, half] = x_ref[at : at + BATCH].astype(bf16)


def mix_of(proj, compress):
    layers = proj.shape[0]
    gap = jnp.zeros((layers, NF - RANK, FIELDS), proj.dtype)
    return jnp.concatenate([jnp.transpose(proj, (0, 2, 1)), gap, compress], axis=1)


def counts_kernel(*refs):
    bags_refs, (counts_ref, idx_ref) = refs[:-2], refs[-2:]
    rows, examples = counts_ref.shape
    column, core, pair = (lax.axis_index(name) for name in ("x", "core", "pair"))
    for hop, bags_ref in enumerate(bags_refs):
        coded = bags_ref[...]
        top, low = (coded >> 7) & 1, (coded >> 6) & 1
        shard = (coded >> 8) << 7
        whole = ((top ^ core) << 10) | shard | (coded & 127)
        partial = jnp.where(top == (column & 1), ((low ^ core) << 10) | shard | (coded & 63), -1)
        spot = jnp.where(coded < DEAD, jnp.where(pair == 0, whole, partial), -1)
        each = coded.shape[1]
        idx_ref[:, hop * each : hop * each + each] = spot.astype(jnp.float32)
    ids = [
        (lax.broadcasted_iota(jnp.int32, (16, 128), 0) + 16 * i)
        .astype(jnp.float32)
        .astype(jnp.bfloat16)
        for i in range(256 // 16)
    ]
    one = jnp.ones((16, 128), jnp.bfloat16)
    zero = jnp.zeros((16, 128), jnp.bfloat16)

    def per_window(window, carry):
        first = (window * 256).astype(jnp.float32)
        for run in range(examples // 128):
            cut = slice(run * 128, run * 128 + 128)
            slots = idx_ref[:, cut] - first
            keys = [
                jnp.broadcast_to(slots[b : b + 1], (16, 128)).astype(jnp.bfloat16) for b in range(8)
            ]
            for i in range(len(ids)):
                hits = [jnp.where(keys[b] == ids[i], one, zero) for b in range(8)]
                while len(hits) > 1:
                    hits = [hits[k] + hits[k + 1] for k in range(0, len(hits), 2)]
                at = pl.multiple_of(window * 256 + i * 16, 16)
                counts_ref[pl.ds(at, 16), cut] = hits[0]
        return carry

    lax.fori_loop(0, rows // 256, per_window, 0)


def by_column(first_ref, last_ref):
    each = last_ref.shape[1]
    column = lax.axis_index("x")
    for hop in range(COLUMNS):
        ref, at = (first_ref, hop * each) if hop < COLUMNS - 1 else (last_ref, 0)
        yield ref, slice(at, at + each), (column + hop) & (COLUMNS - 1)


def pool_kernel(first_ref, last_ref, mine_ref, other_ref, pools_ref):
    share = first_ref.shape[0] // 2
    zs, ys, _, pairs = pools_ref.shape[:4]
    for ref, cut, column in by_column(first_ref, last_ref):
        total = dot(ref[:share, cut], mine_ref[...].reshape(share, WIDTH), ((0,), (0,)))
        total += dot(ref[share:, cut], other_ref[...].reshape(share, WIDTH), ((0,), (0,)))
        total = total.astype(jnp.bfloat16).reshape(ys, zs, pairs, BATCH, WIDTH)
        for y in range(ys):
            for z in range(zs):
                pools_ref[z, y, column] = total[y, z]


def grads_kernel(side, first_ref, last_ref, moved_ref, out_ref):
    share = first_ref.shape[0] // 2
    zs, ys, _, pairs = moved_ref.shape[:4]
    total = jnp.zeros((share, WIDTH), jnp.float32)
    for ref, cut, column in by_column(first_ref, last_ref):
        parts = [
            moved_ref[z, y, column].reshape(pairs * BATCH, WIDTH)
            for y in range(ys)
            for z in range(zs)
        ]
        grads = jnp.concatenate(parts, axis=0)
        total += dot(ref[side * share : side * share + share, cut], grads, ((1,), (0,)))
    out_ref[...] = total.astype(jnp.bfloat16).reshape(out_ref.shape)


def add_kernel(left_ref, right_ref, out_ref):
    for at in range(out_ref.shape[0]):
        total = left_ref[at].astype(jnp.float32) + right_ref[at].astype(jnp.float32)
        out_ref[at] = total.astype(jnp.bfloat16)


def swap(values, axes):
    return lax.all_to_all(values, axes, split_axis=0, concat_axis=0, tiled=True)


def call(kernel, out_shape, ins, args, scratch=(), limit=VMEM_LIMIT):
    vmem = pl.BlockSpec(memory_space=pltpu.VMEM)
    smem = pl.BlockSpec(memory_space=pltpu.SMEM)
    hbm = pl.BlockSpec(memory_space=pltpu.HBM)
    many = isinstance(out_shape, tuple)
    return pl.pallas_call(
        kernel,
        out_shape=out_shape,
        in_specs=[{"s": smem, "v": vmem, "h": hbm}[kind] for kind in ins],
        out_specs=(vmem,) * len(out_shape) if many else vmem,
        scratch_shapes=list(scratch),
        compiler_params=pltpu.CompilerParams(vmem_limit_bytes=limit),
    )(*args)


def per_device(
    table_rows, bag_rows, bag_lens, labels, proj, mlp_in, mlp_out, compress, gain_fm, gain_out, head
):
    f32, bf16 = jnp.float32, jnp.bfloat16
    shape = jax.ShapeDtypeStruct
    tables, rows_dev, width = table_rows.shape
    layers = proj.shape[0]
    column, core = lax.axis_index("x"), lax.axis_index("core")
    quads, pairs, groups, reps, across = 4, 2, 8, 8, [(0, 1), (1, 0)]
    share = rows_dev // 2
    owners = groups * pairs
    piece = shape((quads * pairs, share, width), bf16)
    per_owner = shape((2, 4, COLUMNS, pairs, BATCH, width), bf16)
    exchange = ("zhi", "y", "x", "pair")

    def swap_owners(values):
        flat = values.reshape(COLUMNS * owners, BATCH, width)
        return swap(flat, exchange).reshape(per_owner.shape)

    def of_table(table, first, count):
        return lax.dynamic_slice(table_rows, (table, first, 0), (1, count, width))

    whole = of_table(column, core * share, share)
    half = of_table(
        COLUMNS + column // 2, (column & 1) * share + core * (share // 2), share // 2
    )
    both = jnp.concatenate([whole, jnp.pad(half, ((0, 0), (0, share // 2), (0, 0)))])
    gathered = swap(
        jnp.broadcast_to(both, (quads, *both.shape)).reshape(piece.shape), SUB
    )
    coded = call(
        pick_kernel,
        (shape((8, owners * BATCH), jnp.int32),) * COLUMNS,
        "hh",
        (jnp.transpose(bag_rows, (1, 2, 0)), jnp.transpose(bag_lens)),
        [
            pltpu.VMEM((tables, 8, bag_rows.shape[0]), jnp.int32),
            pltpu.VMEM((tables, bag_rows.shape[0]), jnp.int32),
            pltpu.VMEM((tables, 8, owners * BATCH), jnp.int32),
            pltpu.SemaphoreType.DMA((2,)),
        ],
    )
    bags = [coded[0]] + [
        lax.ppermute(coded[hop], "x", [((i + hop) % COLUMNS, i) for i in range(COLUMNS)])
        for hop in range(1, COLUMNS)
    ]
    each = owners * BATCH

    def count(bags):
        examples = len(bags) * each
        return call(
            counts_kernel,
            shape((8 * rows_dev, examples), bf16),
            "v" * len(bags),
            bags,
            [pltpu.VMEM((8, examples), f32)],
        )

    first = count(bags[:-1])
    gathered, first, late = lax.optimization_barrier((gathered, first, bags[-1]))
    other = lax.ppermute(gathered, "core", across)
    last = count([late])
    other, last, mix = lax.optimization_barrier((other, last, mix_of(proj, compress)))
    pools = call(pool_kernel, per_owner, "vvvv", (first, last, gathered, other))
    near = swap_owners(pools)

    rows = FIELDS * BATCH
    losses, back = call(
        dense_kernel,
        (shape((1, BATCH), f32), shape(near.shape, bf16)),
        "v" * 8,
        (
            labels.reshape(1, BATCH),
            near,
            mix,
            gain_fm,
            mlp_in,
            mlp_out,
            gain_out,
            head,
        ),
        [
            pltpu.VMEM((rows, WIDTH), f32),
            pltpu.VMEM((rows, WIDTH), f32),
            pltpu.VMEM((layers, rows, WIDTH), f32),
            pltpu.VMEM((layers, rows, 1), f32),
            pltpu.VMEM((layers + 1, rows, WIDTH), bf16),
            pltpu.VMEM((rows, WIDTH), bf16),
        ],
    )

    returned = swap_owners(back)
    operands = (first, last, returned)
    other = call(functools.partial(grads_kernel, 1), piece, "vvv", operands)
    other = lax.ppermute(other, "core", across)
    mine = call(functools.partial(grads_kernel, 0), piece, "vvv", operands)
    pieces = swap(call(add_kernel, piece, "vv", (mine, other)), SUB)
    whole, half = jnp.sum(
        pieces.reshape(quads, pairs, share, width).astype(f32), axis=0
    ).astype(bf16)
    own = jnp.concatenate([whole, half[: share // 2]])
    spread = swap(jnp.broadcast_to(own, (reps, *own.shape)), REP)
    row_grads = jnp.concatenate(
        [
            spread[:, :share].reshape(COLUMNS, rows_dev, width),
            spread[:, share:].reshape(COLUMNS // 2, rows_dev, width),
        ]
    )
    return (losses.reshape(BATCH), row_grads.astype(f32))


def solution(mesh):
    view = Mesh(
        mesh.devices.reshape(4, 2, 4, 2, 4, 2), ("x", "core", "y", "zhi", "quad", "pair")
    )
    return jax.shard_map(
        per_device,
        mesh=view,
        in_specs=(
            P(GRP, SUB, None),
            P(REP, GRP, None),
            P(REP, GRP),
            P(REP + GRP + SUB),
            P(),
            P(),
            P(),
            P(),
            P(),
            P(),
            P(),
        ),
        out_specs=(P(REP + GRP + SUB), P(GRP, SUB, None)),
        check_vma=False,
    )
```

```python
import functools

import jax
import jax.numpy as jnp
from jax import lax
from jax.experimental import pallas as pl
from jax.experimental.pallas import tpu as pltpu
from jax.sharding import Mesh
from jax.sharding import PartitionSpec as P

REP = ("x", "core")
GRP = ("y", "zhi")
SUB = ("quad", "pair")
DEAD = 4095
COLUMNS = 4
HOPS = (0, 1, 3, 2)
FIELDS, BATCH, WIDTH, RANK, NF = 48, 16, 128, 8, 12
VMEM_LIMIT = 20 * 1024 * 1024


def pick_kernel(rows_hbm, lens_hbm, *refs):
    outs, (rows_ref, lens_ref, kept_ref, sems) = refs[:COLUMNS], refs[COLUMNS:]
    fetches = [
        pltpu.make_async_copy(rows_hbm, rows_ref, sems.at[0]),
        pltpu.make_async_copy(lens_hbm, lens_ref, sems.at[1]),
    ]
    for fetch in fetches:
        fetch.start()
    for fetch in fetches:
        fetch.wait()
    bag = rows_ref.shape[1]
    slots = lax.broadcasted_iota(jnp.int32, (bag, 128), 0)
    lanes = lax.broadcasted_iota(jnp.int32, (bag, 128), 1)
    column, quad, pair = (lax.axis_index(name) for name in ("x",) + SUB)
    for table in range(rows_ref.shape[0]):
        for group in range(2):
            kept = jnp.zeros((bag, 128), jnp.int32)
            for run in range(4):
                at = (group * 4 + run) * 128
                cut = slice(at, at + 128)
                coded = jnp.where(
                    slots < lens_ref[table : table + 1, cut], rows_ref[table, :, cut], DEAD
                )
                moved = pltpu.roll(coded, (run * 32 - quad * 32) & 127, 1)
                kept = jnp.where(lanes // 32 == run, moved, kept)
            kept_ref[table, :, group * 128 : group * 128 + 128] = kept
    for at, hop in enumerate(HOPS):
        target = (column - hop) & (COLUMNS - 1)
        outs[at][...] = kept_ref[jnp.where(pair == 0, target, COLUMNS + (target >> 1))]


def dot(a, b, dims):
    return lax.dot_general(a, b, (dims, ((), ())), preferred_element_type=jnp.float32)


def slide(values, shift):
    halves = []
    for half in range(2):
        part = values[half * 8 : half * 8 + 8]
        base = (shift + half * 64) % WIDTH
        if base + 7 * RANK >= WIDTH:
            part, base = pltpu.roll(part, base, 1), 0
        halves.append(pltpu.roll(part, base, 1, stride=RANK, stride_axis=0))
    return jnp.concatenate(halves, axis=0)


def dense_kernel(
    labels_ref, near_ref, mix_ref, gain_fm_ref, mlp_in_ref, mlp_out_ref, gain_out_ref, head_ref,
    loss_ref, back_ref,
    x_ref, t_ref, xhat_ref, rstd_ref, xb_ref, d_ref,
):
    f32, bf16 = jnp.float32, jnp.bfloat16
    layers = mix_ref.shape[0]
    rows = FIELDS * BATCH
    chunk = 128
    lane = lax.broadcasted_iota(jnp.int32, (BATCH, WIDTH), 1) // RANK
    zs, ys = near_ref.shape[:2]
    groups = ys * zs
    tables = FIELDS // groups
    for group in range(groups):
        for table in range(tables):
            if table < COLUMNS:
                whole = near_ref[group % zs, group // zs, table, 0]
            else:
                first = 2 * (table - COLUMNS)
                halves = near_ref.at[group % zs, group // zs]
                whole = halves[first, 1].astype(f32) + halves[first + 1, 1].astype(f32)
            at = (group * tables + table) * BATCH
            xb_ref[0, at : at + BATCH] = whole.astype(bf16)
    x_ref[...] = xb_ref[0].astype(f32)

    def example(ref, e):
        return ref[pl.ds(e, FIELDS, stride=BATCH), :]

    saved = []
    for layer in range(layers):
        across = jnp.concatenate([example(x_ref, e).astype(bf16) for e in range(BATCH)], axis=1)
        mixed = dot(mix_ref[layer], across, ((1,), (0,)))
        for e in range(BATCH):
            t_ref[pl.ds(e, FIELDS, stride=BATCH), :] = mixed[:, e * WIDTH : (e + 1) * WIDTH]
        pieces = [mixed[:RANK, e * WIDTH : (e + 1) * WIDTH] for e in range(BATCH)]
        summary = jnp.concatenate(pieces, axis=0).astype(bf16)
        mirrored = jnp.concatenate(pieces[::-1], axis=0).astype(bf16)
        pairs = dot(xb_ref[layer], mirrored, ((1,), (1,)))
        flat = []
        for q in range(FIELDS // BATCH):
            acc = jnp.zeros((BATCH, WIDTH), f32)
            for j in range(BATCH):
                at = (q * BATCH + j) * BATCH
                moved = slide(pairs[at : at + BATCH], (j + 1) * RANK)
                acc = jnp.where(lane == j, moved, acc)
            flat.append(acc)
        flat = jnp.concatenate(flat, axis=1)
        center = jnp.mean(flat, axis=1, keepdims=True)
        flat = flat - center
        rstd_fm = lax.rsqrt(jnp.mean(flat * flat, axis=1, keepdims=True) + 1e-05)
        nhat = flat * rstd_fm
        normed = (nhat * gain_fm_ref[layer : layer + 1]).astype(bf16)
        z = dot(normed, mlp_in_ref[layer], ((1,), (0,)))
        gate = jax.nn.sigmoid(z)
        hidden = (z * gate).astype(bf16)
        machine = dot(hidden, mlp_out_ref[layer], ((1,), (0,)))
        for n in range(NF):
            t_ref[n * BATCH : (n + 1) * BATCH] = machine[:, n * WIDTH : (n + 1) * WIDTH]
        gain = gain_out_ref[layer : layer + 1]
        for at in range(0, rows, chunk):
            cut = slice(at, at + chunk)
            total = t_ref[cut] + x_ref[cut]
            total = total - jnp.mean(total, axis=1, keepdims=True)
            rstd = lax.rsqrt(jnp.mean(total * total, axis=1, keepdims=True) + 1e-05)
            xhat = total * rstd
            xhat_ref[layer, cut] = xhat
            rstd_ref[layer, cut] = rstd
            out = (xhat * gain).astype(bf16)
            xb_ref[layer + 1, cut] = out
            x_ref[cut] = out.astype(f32)
        saved.append((summary, nhat, rstd_fm, z, gate))

    acc = jnp.zeros((BATCH, WIDTH), f32)
    head = head_ref[...].astype(f32)
    for t in range(FIELDS):
        acc = acc + x_ref[t * BATCH : (t + 1) * BATCH] * head[t : t + 1]
    logit = jnp.sum(acc, axis=1, keepdims=True)
    square = (BATCH, BATCH)
    same = lax.broadcasted_iota(jnp.int32, square, 0) == lax.broadcasted_iota(jnp.int32, square, 1)
    labels = jnp.sum(
        jnp.where(same, jnp.broadcast_to(labels_ref[...], square), 0.0), axis=1, keepdims=True
    )
    loss = jnp.maximum(logit, 0.0) + jnp.log1p(jnp.exp(-jnp.abs(logit))) - labels * logit
    loss_ref[...] = jnp.sum(
        jnp.where(same, jnp.broadcast_to(loss, square), 0.0), axis=0, keepdims=True
    )
    dlogit = jnp.broadcast_to(jax.nn.sigmoid(logit) - labels, (BATCH, WIDTH))
    for t in range(FIELDS):
        x_ref[t * BATCH : (t + 1) * BATCH] = (dlogit * head[t : t + 1]).astype(bf16).astype(f32)

    low = lax.broadcasted_iota(jnp.int32, (RANK, WIDTH), 0) >= NF - RANK
    for layer in reversed(range(layers)):
        summary, nhat, rstd_fm, z, gate = saved[layer]
        gain = gain_out_ref[layer : layer + 1]
        for at in range(0, rows, chunk):
            cut = slice(at, at + chunk)
            xhat = xhat_ref[layer, cut]
            dxhat = x_ref[cut] * gain
            mean_d = jnp.mean(dxhat, axis=1, keepdims=True)
            mean_p = jnp.mean(dxhat * xhat, axis=1, keepdims=True)
            t_ref[cut] = rstd_ref[layer, cut] * (dxhat - mean_d - xhat * mean_p)
        dmachine = jnp.concatenate(
            [t_ref[n * BATCH : (n + 1) * BATCH].astype(bf16) for n in range(NF)], axis=1
        )
        dhidden = dot(dmachine, mlp_out_ref[layer], ((1,), (1,))).astype(bf16).astype(f32)
        dz = (dhidden * gate * (1.0 + z * (1.0 - gate))).astype(bf16)
        dnormed = dot(dz, mlp_in_ref[layer], ((1,), (1,))).astype(bf16).astype(f32)
        dnhat = dnormed * gain_fm_ref[layer : layer + 1]
        mean_d = jnp.mean(dnhat, axis=1, keepdims=True)
        mean_p = jnp.mean(dnhat * nhat, axis=1, keepdims=True)
        dflat = rstd_fm * (dnhat - mean_d - nhat * mean_p)
        for q in range(FIELDS // BATCH):
            part = dflat[:, q * WIDTH : (q + 1) * WIDTH]
            for j in range(BATCH):
                at = (q * BATCH + j) * BATCH
                only = jnp.where(lane == j, part, 0.0)
                d_ref[at : at + BATCH] = slide(only, -j * RANK).astype(bf16)
        dpairs = d_ref[...]
        dsummary = dot(dpairs, xb_ref[layer], ((0,), (0,)))
        parts = []
        for e in range(BATCH):
            straight = example(t_ref, e)
            parts.append(
                jnp.concatenate(
                    [
                        dsummary[e * RANK : (e + 1) * RANK],
                        jnp.where(low, straight[RANK : 2 * RANK], 0.0),
                        straight[2 * RANK :],
                    ],
                    axis=0,
                ).astype(bf16)
            )
        dacross = dot(mix_ref[layer], jnp.concatenate(parts, axis=1), ((0,), (0,)))
        for e in range(BATCH):
            x_ref[pl.ds(e, FIELDS, stride=BATCH), :] = dacross[:, e * WIDTH : (e + 1) * WIDTH]
        for at in range(0, rows, chunk):
            cut = slice(at, at + chunk)
            dx = x_ref[cut] + t_ref[cut] + dot(d_ref[cut], summary, ((1,), (0,)))
            x_ref[cut] = dx.astype(bf16).astype(f32)

    for group in range(groups):
        for column in range(COLUMNS):
            for half, table in enumerate((column, COLUMNS + column // 2)):
                at = (group * tables + table) * BATCH
                back_ref[group % zs, group // zs, column, half] = x_ref[at : at + BATCH].astype(bf16)


def mix_of(proj, compress):
    layers = proj.shape[0]
    gap = jnp.zeros((layers, NF - RANK, FIELDS), proj.dtype)
    return jnp.concatenate([jnp.transpose(proj, (0, 2, 1)), gap, compress], axis=1)


def counts_kernel(*refs):
    bags_refs, (counts_ref, idx_ref) = refs[:-2], refs[-2:]
    rows, examples = counts_ref.shape
    column, core, pair = (lax.axis_index(name) for name in ("x", "core", "pair"))
    for hop, bags_ref in enumerate(bags_refs):
        coded = bags_ref[...]
        top, low = (coded >> 7) & 1, (coded >> 6) & 1
        shard = (coded >> 8) << 7
        whole = ((top ^ core) << 10) | shard | (coded & 127)
        partial = jnp.where(top == (column & 1), ((low ^ core) << 10) | shard | (coded & 63), -1)
        spot = jnp.where(coded < DEAD, jnp.where(pair == 0, whole, partial), -1)
        each = coded.shape[1]
        idx_ref[:, hop * each : hop * each + each] = spot.astype(jnp.float32)
    ids = [
        (lax.broadcasted_iota(jnp.int32, (16, 128), 0) + 16 * i)
        .astype(jnp.float32)
        .astype(jnp.bfloat16)
        for i in range(256 // 16)
    ]
    one = jnp.ones((16, 128), jnp.bfloat16)
    zero = jnp.zeros((16, 128), jnp.bfloat16)

    def per_window(window, carry):
        first = (window * 256).astype(jnp.float32)
        for run in range(examples // 128):
            cut = slice(run * 128, run * 128 + 128)
            slots = idx_ref[:, cut] - first
            keys = [
                jnp.broadcast_to(slots[b : b + 1], (16, 128)).astype(jnp.bfloat16) for b in range(8)
            ]
            for i in range(len(ids)):
                hits = [jnp.where(keys[b] == ids[i], one, zero) for b in range(8)]
                while len(hits) > 1:
                    hits = [hits[k] + hits[k + 1] for k in range(0, len(hits), 2)]
                at = pl.multiple_of(window * 256 + i * 16, 16)
                counts_ref[pl.ds(at, 16), cut] = hits[0]
        return carry

    lax.fori_loop(0, rows // 256, per_window, 0)


def by_column(first_ref, last_ref):
    each = last_ref.shape[1]
    column = lax.axis_index("x")
    for i, hop in enumerate(HOPS):
        ref, at = (first_ref, i * each) if i < COLUMNS - 1 else (last_ref, 0)
        yield ref, slice(at, at + each), (column + hop) & (COLUMNS - 1)


def pool_kernel(first_ref, last_ref, mine_ref, other_ref, pools_ref):
    share = first_ref.shape[0] // 2
    zs, ys, _, pairs = pools_ref.shape[:4]
    for ref, cut, column in by_column(first_ref, last_ref):
        total = dot(ref[:share, cut], mine_ref[...].reshape(share, WIDTH), ((0,), (0,)))
        total += dot(ref[share:, cut], other_ref[...].reshape(share, WIDTH), ((0,), (0,)))
        total = total.astype(jnp.bfloat16).reshape(ys, zs, pairs, BATCH, WIDTH)
        for y in range(ys):
            for z in range(zs):
                pools_ref[z, y, column] = total[y, z]


def grads_kernel(side, first_ref, last_ref, moved_ref, out_ref):
    share = first_ref.shape[0] // 2
    zs, ys, _, pairs = moved_ref.shape[:4]
    total = jnp.zeros((share, WIDTH), jnp.float32)
    for ref, cut, column in by_column(first_ref, last_ref):
        parts = [
            moved_ref[z, y, column].reshape(pairs * BATCH, WIDTH)
            for y in range(ys)
            for z in range(zs)
        ]
        grads = jnp.concatenate(parts, axis=0)
        total += dot(ref[side * share : side * share + share, cut], grads, ((1,), (0,)))
    out_ref[...] = total.astype(jnp.bfloat16).reshape(out_ref.shape)


def add_kernel(left_ref, right_ref, out_ref):
    for at in range(out_ref.shape[0]):
        total = left_ref[at].astype(jnp.float32) + right_ref[at].astype(jnp.float32)
        out_ref[at] = total.astype(jnp.bfloat16)


def swap(values, axes):
    return lax.all_to_all(values, axes, split_axis=0, concat_axis=0, tiled=True)


def call(kernel, out_shape, ins, args, scratch=(), limit=VMEM_LIMIT):
    vmem = pl.BlockSpec(memory_space=pltpu.VMEM)
    smem = pl.BlockSpec(memory_space=pltpu.SMEM)
    hbm = pl.BlockSpec(memory_space=pltpu.HBM)
    many = isinstance(out_shape, tuple)
    return pl.pallas_call(
        kernel,
        out_shape=out_shape,
        in_specs=[{"s": smem, "v": vmem, "h": hbm}[kind] for kind in ins],
        out_specs=(vmem,) * len(out_shape) if many else vmem,
        scratch_shapes=list(scratch),
        compiler_params=pltpu.CompilerParams(vmem_limit_bytes=limit),
    )(*args)


def per_device(
    table_rows, bag_rows, bag_lens, labels, proj, mlp_in, mlp_out, compress, gain_fm, gain_out, head
):
    f32, bf16 = jnp.float32, jnp.bfloat16
    shape = jax.ShapeDtypeStruct
    tables, rows_dev, width = table_rows.shape
    layers = proj.shape[0]
    column, core = lax.axis_index("x"), lax.axis_index("core")
    quads, pairs, groups, reps, across = 4, 2, 8, 8, [(0, 1), (1, 0)]
    share = rows_dev // 2
    owners = groups * pairs
    piece = shape((quads * pairs, share, width), bf16)
    per_owner = shape((2, 4, COLUMNS, pairs, BATCH, width), bf16)
    exchange = ("zhi", "y", "x", "pair")

    def swap_owners(values):
        flat = values.reshape(COLUMNS * owners, BATCH, width)
        return swap(flat, exchange).reshape(per_owner.shape)

    def of_table(table, first, count):
        return lax.dynamic_slice(table_rows, (table, first, 0), (1, count, width))

    whole = of_table(column, core * share, share)
    half = of_table(
        COLUMNS + column // 2, (column & 1) * share + core * (share // 2), share // 2
    )
    both = jnp.concatenate([whole, jnp.pad(half, ((0, 0), (0, share // 2), (0, 0)))])
    gathered = swap(
        jnp.broadcast_to(both, (quads, *both.shape)).reshape(piece.shape), SUB
    )
    coded = call(
        pick_kernel,
        (shape((8, owners * BATCH), jnp.int32),) * COLUMNS,
        "hh",
        (jnp.transpose(bag_rows, (1, 2, 0)), jnp.transpose(bag_lens)),
        [
            pltpu.VMEM((tables, 8, bag_rows.shape[0]), jnp.int32),
            pltpu.VMEM((tables, bag_rows.shape[0]), jnp.int32),
            pltpu.VMEM((tables, 8, owners * BATCH), jnp.int32),
            pltpu.SemaphoreType.DMA((2,)),
        ],
    )
    bags = [coded[0]] + [
        lax.ppermute(mine, "x", [((i + hop) % COLUMNS, i) for i in range(COLUMNS)])
        for mine, hop in zip(coded[1:], HOPS[1:])
    ]
    each = owners * BATCH

    def count(bags):
        examples = len(bags) * each
        return call(
            counts_kernel,
            shape((8 * rows_dev, examples), bf16),
            "v" * len(bags),
            bags,
            [pltpu.VMEM((8, examples), f32)],
        )

    first = count(bags[:-1])
    gathered, first, late = lax.optimization_barrier((gathered, first, bags[-1]))
    other = lax.ppermute(gathered, "core", across)
    last = count([late])
    other, last, mix = lax.optimization_barrier((other, last, mix_of(proj, compress)))
    pools = call(pool_kernel, per_owner, "vvvv", (first, last, gathered, other))
    near = swap_owners(pools)

    rows = FIELDS * BATCH
    losses, back = call(
        dense_kernel,
        (shape((1, BATCH), f32), shape(near.shape, bf16)),
        "v" * 8,
        (
            labels.reshape(1, BATCH),
            near,
            mix,
            gain_fm,
            mlp_in,
            mlp_out,
            gain_out,
            head,
        ),
        [
            pltpu.VMEM((rows, WIDTH), f32),
            pltpu.VMEM((rows, WIDTH), f32),
            pltpu.VMEM((layers, rows, WIDTH), f32),
            pltpu.VMEM((layers, rows, 1), f32),
            pltpu.VMEM((layers + 1, rows, WIDTH), bf16),
            pltpu.VMEM((rows, WIDTH), bf16),
        ],
    )

    returned = swap_owners(back)
    operands = (first, last, returned)
    other = call(functools.partial(grads_kernel, 1), piece, "vvv", operands)
    other = lax.ppermute(other, "core", across)
    mine = call(functools.partial(grads_kernel, 0), piece, "vvv", operands)
    pieces = swap(call(add_kernel, piece, "vv", (mine, other)), SUB)
    whole, half = jnp.sum(
        pieces.reshape(quads, pairs, share, width).astype(f32), axis=0
    ).astype(bf16)
    own = jnp.concatenate([whole, half[: share // 2]])
    spread = swap(jnp.broadcast_to(own, (reps, *own.shape)), REP)
    row_grads = jnp.concatenate(
        [
            spread[:, :share].reshape(COLUMNS, rows_dev, width),
            spread[:, share:].reshape(COLUMNS // 2, rows_dev, width),
        ]
    )
    return (losses.reshape(BATCH), row_grads.astype(f32))


def solution(mesh):
    view = Mesh(
        mesh.devices.reshape(4, 2, 4, 2, 4, 2), ("x", "core", "y", "zhi", "quad", "pair")
    )
    return jax.shard_map(
        per_device,
        mesh=view,
        in_specs=(
            P(GRP, SUB, None),
            P(REP, GRP, None),
            P(REP, GRP),
            P(REP + GRP + SUB),
            P(),
            P(),
            P(),
            P(),
            P(),
            P(),
            P(),
        ),
        out_specs=(P(REP + GRP + SUB), P(GRP, SUB, None)),
        check_vma=False,
    )
```
